32 devices in a mesh: clip: 4 (over y, core), seq: 4 (over z), tp: 2 (over x).
Axes of the slice: x: 2, y: 2, z: 4, core: 2. Of those that a mesh axis runs over, the one named last changes fastest.
Arguments:
- frames: bfloat16 [768, 16, 1152], P('tp', ('clip', 'seq')), parts along dimension 1, may hold values from -6 to 6
- timestep: int32 [4], P('clip'), parts along dimension 0, may hold values from 0 to 999
- embed_weight: bfloat16 [256, 1152], replicated, may hold values from -0.375 to 0.375
- block_weight: bfloat16 [1152, 3456], P(('seq', 'tp')), may hold values from -0.1875 to 0.1875
- spatial_table: float32 [3, 1152], replicated, may hold values from -3 to 3
- temporal_table: float32 [3, 1152], replicated, may hold values from -3 to 3
- spatial_qkv: bfloat16 [1152, 3, 1152], P(None, None, 'tp'), may hold values from -1 to 1
- spatial_out: bfloat16 [1152, 1152], P('tp'), may hold values from -0.1875 to 0.1875
- temporal_qkv: bfloat16 [1152, 3, 1152], P(None, None, 'tp'), may hold values from -1 to 1
- temporal_out: bfloat16 [1152, 1152], P('tp'), may hold values from -0.1875 to 0.1875
Outputs:
- mixed: float32 [768, 16, 1152], P('tp', ('clip', 'seq')), parts along dimension 1
The draws below stay inside these ranges and needn't reach their ends.
There are 4 independent parts, one for each index of `clip`. The reference program is written for one: setup_inputs(seed, part) draws one part's arguments, and reference() takes and returns one part's arrays. A program takes and returns all parts, laid end to end along the dimension named above; an argument that names none is the same for every part. Nothing has to cross between parts.
All inputs are finite; a program needn't handle non-finite values.
Results may differ from the reference program's by a relative error of at most 0.0085.
Values may be sent and summed in bfloat16 or wider, within the bound.
A program may use at most 128 MiB of HBM per device.

```python
import math
import jax
import jax.numpy as jnp
from jax import lax

D = 1152
HEADS = 16
HEAD_DIM = 72
FREQ = 256
SPATIAL = 768
FRAMES = 4


def draw_spatial_qkv(key, part):
    key = jax.random.fold_in(key, 11)
    return jnp.clip(jax.random.normal(key, (D, 3, D), jnp.float32) / math.sqrt(D), -1.0, 1.0).astype(jnp.bfloat16)


def draw_temporal_qkv(key, part):
    key = jax.random.fold_in(key, 12)
    return jnp.clip(jax.random.normal(key, (D, 3, D), jnp.float32) / math.sqrt(D), -1.0, 1.0).astype(jnp.bfloat16)


def block_scale(own_key, extent, shards, least, high):
    loudness = 1.0
    for position, shards_of in shards:
        draws = jax.random.uniform(jax.random.fold_in(jax.random.fold_in(own_key, 6), position), (shards_of,), jnp.float32, least / len(shards), high / len(shards))
        loudness = loudness * jnp.repeat(jnp.exp(draws), extent[position] // shards_of).reshape((-1,) + (1,) * (len(extent) - 1 - position))
    return loudness


def gaussian(key, extent, deviation, limit, shards=(), kind=jnp.bfloat16):
    level = block_scale(key, extent, shards, -0.22, 0.18) if shards else 1.0
    values = jax.random.normal(key, extent, jnp.float32) * deviation * level
    return jnp.minimum(jnp.maximum(values, -limit), limit).astype(kind)


def setup_inputs(seed: int = 0, part: int = 0) -> dict:
    arg_keys = jax.random.split(jax.random.key(seed), 11)
    part_splits = jax.random.split(jax.random.fold_in(arg_keys[10], part), 11)
    return {
        "frames": gaussian(part_splits[0], (SPATIAL, FRAMES, D), 1.0, 6.0, ((0, 2), (1, 4))),
        "timestep": jax.random.randint(part_splits[1], (1,), 0, 1000).astype(jnp.int32),
        "embed_weight": gaussian(arg_keys[2], (FREQ, D), FREQ ** -0.5, 0.375),
        "block_weight": gaussian(arg_keys[3], (D, 3 * D), D ** -0.5, 0.1875, ((0, 8),)),
        "spatial_table": gaussian(arg_keys[4], (3, D), 0.5, 3.0, (), jnp.float32),
        "temporal_table": gaussian(arg_keys[5], (3, D), 0.5, 3.0, (), jnp.float32),
        "spatial_qkv": draw_spatial_qkv(jax.random.fold_in(arg_keys[10], 71), part),
        "spatial_out": gaussian(arg_keys[7], (D, D), D ** -0.5, 0.1875, ((0, 2),)),
        "temporal_qkv": draw_temporal_qkv(jax.random.fold_in(arg_keys[10], 71), part),
        "temporal_out": gaussian(arg_keys[9], (D, D), D ** -0.5, 0.1875, ((0, 2),)),
    }


def layer_norm(values):
    mean = lax.optimization_barrier(jnp.mean(values, axis=-1, keepdims=True))
    centred = values - mean
    variance = lax.optimization_barrier(jnp.mean(centred * centred, axis=-1, keepdims=True))
    return centred * lax.rsqrt(variance + 1e-06)

def modulate(tokens, mods):
    normed = layer_norm(tokens.astype(jnp.float32))
    return (normed * (1.0 + mods[1]) + mods[0]).astype(jnp.bfloat16)

def residual_add(tokens, mods, projected):
    return tokens.astype(jnp.float32) + mods[2] * projected

def soft_weights(scores):
    peak = lax.optimization_barrier(jnp.max(scores, axis=-1, keepdims=True))
    raised = jnp.exp(scores - peak)
    return (raised / lax.optimization_barrier(jnp.sum(raised, axis=-1, keepdims=True))).astype(jnp.bfloat16)

def time_features(timestep):
    half = FREQ // 2
    ladder = jnp.exp(-math.log(10000.0) * jnp.arange(half, dtype=jnp.float32) / half)
    angles = timestep.astype(jnp.float32)[:, None] * ladder[None, :]
    return jnp.concatenate([jnp.cos(angles), jnp.sin(angles)], axis=-1)

def project(attended, out_weight):
    return jnp.dot(attended, out_weight, preferred_element_type=jnp.float32)

def reference(frames, timestep, embed_weight, block_weight, spatial_table, temporal_table, spatial_qkv, spatial_out, temporal_qkv, temporal_out):
    features = time_features(timestep)
    embedded = jax.nn.silu(jnp.dot(features, embed_weight.astype(jnp.float32), precision=lax.Precision.HIGHEST))
    modulation = jnp.dot(embedded, block_weight.astype(jnp.float32), precision=lax.Precision.HIGHEST).reshape(3, D)
    spatial_mods = spatial_table + modulation
    temporal_mods = temporal_table + modulation
    factor = 1.0 / math.sqrt(HEAD_DIM)

    def one_frame(tokens):
        normed = modulate(tokens, spatial_mods)
        qkv = jnp.dot(normed, spatial_qkv.reshape(D, 3 * D), preferred_element_type=jnp.float32).astype(jnp.bfloat16)
        grid = qkv.reshape(SPATIAL, 3, HEADS, HEAD_DIM).astype(jnp.float32)
        scores = jnp.einsum('qhd,khd->hqk', grid[:, 0], grid[:, 1]) * factor
        weights = soft_weights(scores)
        attended = jnp.einsum('hqk,khd->qhd', weights.astype(jnp.float32), grid[:, 2])
        attended = attended.astype(jnp.bfloat16).reshape(SPATIAL, D)
        return residual_add(tokens, spatial_mods, project(attended, spatial_out))
    by_frame = jnp.swapaxes(frames, 0, 1)
    middle = jnp.swapaxes(lax.map(one_frame, by_frame), 0, 1)
    normed = modulate(middle, temporal_mods)
    qkv = jnp.dot(normed, temporal_qkv.reshape(D, 3 * D), preferred_element_type=jnp.float32).astype(jnp.bfloat16)
    grid = qkv.reshape(SPATIAL, FRAMES, 3, HEADS, HEAD_DIM).astype(jnp.float32)
    scores = jnp.einsum('pfhd,pghd->phfg', grid[:, :, 0], grid[:, :, 1]) * factor
    weights = soft_weights(scores)
    attended = jnp.einsum('phfg,pghd->pfhd', weights.astype(jnp.float32), grid[:, :, 2])
    attended = attended.astype(jnp.bfloat16).reshape(SPATIAL, FRAMES, D)
    return residual_add(middle, temporal_mods, project(attended, temporal_out))
```

```python
import functools
import math

import jax
import jax.numpy as jnp
from jax import lax
from jax.experimental import pallas as pl
from jax.experimental.pallas import tpu as pltpu
from jax.sharding import PartitionSpec as P

HEAD_DIM = 72
FREQ = 256
F32 = jnp.float32
BF16 = jnp.bfloat16
MESH = pl.DeviceIdType.MESH
NT = (((1,), (1,)), ((), ()))
TN = (((0,), (0,)), ((), ()))
NN = (((1,), (0,)), ((), ()))
FACTOR = 1.0 / math.sqrt(HEAD_DIM)
FACTOR2 = FACTOR * math.log2(math.e)


def time_features(timestep):
    half = FREQ // 2
    ladder = jnp.exp(-math.log(10000.0) * jnp.arange(half, dtype=jnp.float32) / half)
    angles = timestep.astype(jnp.float32)[:, None] * ladder[None, :]
    return jnp.concatenate([jnp.cos(angles), jnp.sin(angles)], axis=-1)


def mm(a, b, dims):
    return lax.dot_general(a, b, dims, preferred_element_type=F32)


def split_rows(row):
    wide = jnp.broadcast_to(row, (8, row.shape[1]))
    first = wide.astype(BF16).astype(F32)
    rest = wide - first
    second = rest.astype(BF16).astype(F32)
    third = rest - second
    index = lax.broadcasted_iota(jnp.int32, wide.shape, 0)
    zero = jnp.zeros_like(wide)
    return jnp.where(
        index == 0, first, jnp.where(index == 1, second, jnp.where(index == 2, third, zero))
    ).astype(BF16)


def normalise(values, scale, shift):
    width = values.shape[1]
    mean = jnp.sum(values, axis=1, keepdims=True) * (1.0 / width)
    centred = values - mean
    variance = jnp.sum(centred * centred, axis=1, keepdims=True) * (1.0 / width)
    return (centred * lax.rsqrt(variance + 1e-06) * (1.0 + scale) + shift).astype(BF16)


def kernel(
    depth,
    feats_ref,
    table_s,
    table_t,
    frames_hbm,
    embed_hbm,
    block_hbm,
    wqs_hbm,
    wos_hbm,
    wqt_hbm,
    wot_hbm,
    out_ref,
    frames,
    embed,
    block,
    wqs,
    wos,
    wqt,
    wot,
    theirs,
    term,
    terms,
    mods_s,
    mods_t,
    qkv,
    att,
    part_send,
    part_recv,
    own,
    middle,
    nt,
    xa,
    xb,
    qkvt,
    attt,
    pb,
    pr,
    po,
    rs,
    rr,
    load_sem,
    term_send,
    term_recv,
    fr_send,
    fr_recv,
    part_ss,
    part_rs,
    nt_send,
    nt_recv,
    fx_send,
    fx_recv,
    pb_send,
    pb_recv,
    rs_send,
    rs_recv,
):
    me_s = lax.axis_index("seq")
    me_t = lax.axis_index("tp")
    peer_t = 1 - me_t
    count, width = frames.shape
    heads = qkv.shape[1]
    pos = nt.shape[1]
    cuts = [(0, 256), (256, count - 256)] if count == 384 else [(0, count)]

    loads = []
    for i, (src, dst) in enumerate(
        [
            (embed_hbm, embed),
            (block_hbm, block),
            (frames_hbm, frames),
            (wqs_hbm, wqs),
            (wos_hbm, wos),
            (wqt_hbm, wqt),
            (wot_hbm, wot),
        ]
    ):
        copy = pltpu.make_async_copy(src, dst, load_sem.at[i])
        copy.start()
        loads.append(copy)

    barrier = pltpu.get_barrier_semaphore()
    peers = [(ds, dt) for ds in range(depth) for dt in range(2) if ds or dt]
    for ds, dt in peers:
        pl.semaphore_signal(
            barrier,
            inc=1,
            device_id={"seq": lax.rem(me_s + ds, depth), "tp": lax.rem(me_t + dt, 2)},
            device_id_type=MESH,
        )
    pl.semaphore_wait(barrier, len(peers))

    frame_copies = []
    for i, (r0, n) in enumerate(cuts):
        copy = pltpu.make_async_remote_copy(
            src_ref=frames_hbm.at[pl.ds(r0, n)],
            dst_ref=theirs.at[pl.ds(r0, n)],
            send_sem=fr_send.at[i],
            recv_sem=fr_recv.at[i],
            device_id={"tp": peer_t},
            device_id_type=MESH,
        )
        copy.start()
        frame_copies.append(copy)

    loads[0].wait()
    hidden = mm(split_rows(feats_ref[...]), embed[...], NN)
    hidden = hidden[0:1] + hidden[1:2] + hidden[2:3]
    hidden = hidden / (1.0 + jnp.exp(-hidden))
    share = block.shape[0]
    start = (me_s * 2 + me_t) * share
    chosen = (
        lax.broadcasted_iota(jnp.int32, (width, share), 0)
        == lax.broadcasted_iota(jnp.int32, (width, share), 1) + start
    )
    mine = mm(split_rows(hidden), chosen.astype(F32).astype(BF16), NN).astype(BF16)
    loads[1].wait()
    spread = mm(mine, block[...], NN)
    spread = spread[0:1] + spread[1:2] + spread[2:3]
    for i in range(3):
        term[i : i + 1, :] = spread[:, i * width : (i + 1) * width]
    term_copies = []
    for i, (ds, dt) in enumerate(peers):
        copy = pltpu.make_async_remote_copy(
            src_ref=term,
            dst_ref=terms.at[i],
            send_sem=term_send.at[i],
            recv_sem=term_recv.at[i],
            device_id={"seq": lax.rem(me_s + ds, depth), "tp": lax.rem(me_t + dt, 2)},
            device_id_type=MESH,
        )
        copy.start()
        term_copies.append(copy)
    total = term[...]
    for i, copy in enumerate(term_copies):
        copy.wait_recv()
        total = total + terms[i]
    mods_s[...] = table_s[...] + total
    mods_t[...] = table_t[...] + total

    def spatial_in(tokens, r0, n, c0):
        normed = jnp.concatenate(
            [
                normalise(
                    tokens[pl.ds(r0 + k, 128), :].astype(F32), mods_s[1:2, :], mods_s[0:1, :]
                )
                for k in range(0, n, 128)
            ],
            axis=0,
        )

        @pl.loop(0, 3)
        def _(j):
            rows = mm(wqs[j], normed, NT)
            qkv[j, :, :, pl.ds(c0, n)] = rows.reshape(heads, HEAD_DIM, n).astype(BF16)

    loads[2].wait()
    loads[3].wait()
    for r0, n in cuts:
        spatial_in(frames, r0, n, r0)
    for i, (r0, n) in enumerate(cuts):
        frame_copies[i].wait_recv()
        spatial_in(theirs, r0, n, count + r0)

    def attend(c0, n):
        @pl.loop(0, heads)
        def _(h):
            scores = mm(qkv[1, h], qkv[0, h, :, pl.ds(c0, n)], TN)
            peak = jnp.max(scores, axis=0, keepdims=True)
            raised = jnp.exp2((scores - peak) * FACTOR2)
            norm = jnp.sum(raised, axis=0, keepdims=True)
            att[h, :, pl.ds(c0, n)] = mm(qkv[2, h], raised.astype(BF16), NN) / norm

    def project(c0, n):
        heads_out = att[:, :, pl.ds(c0, n)].reshape(heads * HEAD_DIM, n).astype(BF16)
        return mm(heads_out, wos[...], TN)

    loads[4].wait()
    part_copies = []
    for i, (r0, n) in enumerate(cuts):
        attend(count + r0, n)
        for k in range(r0, r0 + n, 128):
            part_send[pl.ds(k, 128), :] = project(count + k, 128).astype(BF16)
        copy = pltpu.make_async_remote_copy(
            src_ref=part_send.at[pl.ds(r0, n)],
            dst_ref=part_recv.at[pl.ds(r0, n)],
            send_sem=part_ss.at[i],
            recv_sem=part_rs.at[i],
            device_id={"tp": peer_t},
            device_id_type=MESH,
        )
        copy.start()
        part_copies.append(copy)
    for r0, n in cuts:
        attend(r0, n)
    for k in range(0, count, 128):
        own[pl.ds(k, 128), :] = project(k, 128)

    def seq_copy(src, dst, send, recv, there):
        return pltpu.make_async_remote_copy(
            src_ref=src.at[there],
            dst_ref=dst.at[me_s],
            send_sem=send.at[there],
            recv_sem=recv.at[me_s],
            device_id={"seq": there},
            device_id_type=MESH,
        )

    def seq_arrival(src, dst, send, recv, there):
        return pltpu.make_async_remote_copy(
            src_ref=src.at[there],
            dst_ref=dst.at[there],
            send_sem=send.at[there],
            recv_sem=recv.at[there],
            device_id={"seq": there},
            device_id_type=MESH,
        )

    ready = 0
    for i, (r0, n) in enumerate(cuts):
        part_copies[i].wait_recv()
        for k in range(r0, r0 + n, 128):
            rows = pl.ds(k, 128)
            middle[rows, :] = frames[rows, :].astype(F32) + mods_s[2:3, :] * (
                own[rows, :] + part_recv[rows, :].astype(F32)
            )
        while (ready + 1) * pos <= r0 + n:
            b = ready
            nt[b] = normalise(
                middle[pl.ds(b * pos, pos), :], mods_t[1:2, :], mods_t[0:1, :]
            )

            @pl.when(me_s != b)
            def _():
                seq_copy(nt, xa, nt_send, nt_recv, b).start()

            ready += 1

    def tp_copy(src, dst, send, recv, f):
        return pltpu.make_async_remote_copy(
            src_ref=src.at[f],
            dst_ref=dst.at[f],
            send_sem=send.at[f],
            recv_sem=recv.at[f],
            device_id={"tp": peer_t},
            device_id_type=MESH,
        )

    xa[me_s] = nt[me_s]
    tp_copy(xa, xb, fx_send, fx_recv, me_s).start()
    loads[5].wait()
    loads[6].wait()

    def temporal_in(f):
        tp_copy(xa, xb, fx_send, fx_recv, f).wait_recv()
        if pos % 16:
            both = jnp.concatenate([xa[f].astype(F32), xb[f].astype(F32)], axis=0).astype(BF16)
        else:
            both = jnp.concatenate([xa[f], xb[f]], axis=0)
        for j in range(3):
            rows = mm(wqt[j], both, NT)
            qkvt[j, f] = rows.reshape(heads, HEAD_DIM, 2 * pos).astype(BF16)

    @pl.loop(1, depth)
    def _(d):
        f = lax.rem(me_s + d, depth)
        seq_arrival(nt, xa, nt_send, nt_recv, f).wait_recv()
        tp_copy(xa, xb, fx_send, fx_recv, f).start()
        temporal_in(lax.rem(me_s + d - 1, depth))

    temporal_in(lax.rem(me_s + depth - 1, depth))

    @pl.loop(0, depth)
    def _(d):
        f = lax.rem(me_s + 1 + d, depth)

        @pl.loop(0, heads)
        def _(h):
            query = qkvt[0, f, h].astype(F32)
            scores = [
                jnp.sum(query * qkvt[1, g, h].astype(F32), axis=0, keepdims=True) * FACTOR
                for g in range(depth)
            ]
            peak = functools.reduce(jnp.maximum, scores)
            raised = [jnp.exp(s - peak) for s in scores]
            norm = functools.reduce(jnp.add, raised)
            result = None
            for g in range(depth):
                weight = (raised[g] / norm).astype(BF16).astype(F32)
                piece = weight * qkvt[2, g, h].astype(F32)
                result = piece if result is None else result + piece
            attt[f, h] = result

        flat = attt[f].reshape(heads * HEAD_DIM, 2 * pos).astype(BF16)
        projected = mm(flat, wot[...], TN)
        pb[f] = projected[pos:].astype(BF16)
        tp_copy(pb, pr, pb_send, pb_recv, f).start()
        po[f] = projected[:pos]

    @pl.loop(0, depth)
    def _(d):
        f = lax.rem(me_s + 1 + d, depth)
        tp_copy(pb, pr, pb_send, pb_recv, f).wait_recv()
        rs[f] = (po[f] + pr[f].astype(F32)).astype(BF16)

        @pl.when(d < depth - 1)
        def _():
            seq_copy(rs, rr, rs_send, rs_recv, f).start()

    rr[me_s] = rs[me_s]

    def finish(b):
        rows = pl.ds(pl.multiple_of(b * pos, 8), pos)
        out_ref[rows, :] = middle[rows, :] + mods_t[2:3, :] * rr[b].astype(F32)

    finish(me_s)

    @pl.loop(1, depth)
    def _(d):
        b = lax.rem(me_s + d, depth)
        seq_arrival(rs, rr, rs_send, rs_recv, b).wait_recv()
        finish(b)

    for copy in frame_copies + term_copies + part_copies:
        copy.wait_send()

    @pl.loop(0, depth)
    def _(f):
        tp_copy(xa, xb, fx_send, fx_recv, f).wait_send()
        tp_copy(pb, pr, pb_send, pb_recv, f).wait_send()

        @pl.when(f != me_s)
        def _():
            seq_copy(nt, xa, nt_send, nt_recv, f).wait_send()
            seq_copy(rs, rr, rs_send, rs_recv, f).wait_send()


def body(
    frames,
    timestep,
    embed_weight,
    block_weight,
    spatial_table,
    temporal_table,
    spatial_qkv,
    spatial_out,
    temporal_qkv,
    temporal_out,
):
    depth = lax.axis_size("seq")
    count, _, width = frames.shape
    local = spatial_out.shape[0]
    heads = local // HEAD_DIM
    pos = count // depth
    group = 2 * depth - 1
    vmem = pl.BlockSpec(memory_space=pltpu.VMEM)
    hbm = pl.BlockSpec(memory_space=pl.ANY)
    dma = pltpu.SemaphoreType.DMA
    blocks = pltpu.VMEM((depth, pos, width), BF16)
    result = pl.pallas_call(
        functools.partial(kernel, depth),
        out_shape=jax.ShapeDtypeStruct((count, width), F32),
        in_specs=[vmem] * 3 + [hbm] * 7,
        out_specs=vmem,
        scratch_shapes=[
            pltpu.VMEM((count, width), BF16),
            pltpu.VMEM(embed_weight.shape, BF16),
            pltpu.VMEM(block_weight.shape, BF16),
            pltpu.VMEM((3, local, width), BF16),
            pltpu.VMEM((local, width), BF16),
            pltpu.VMEM((3, local, width), BF16),
            pltpu.VMEM((local, width), BF16),
            pltpu.VMEM((count, width), BF16),
            pltpu.VMEM((3, width), F32),
            pltpu.VMEM((group, 3, width), F32),
            pltpu.VMEM((3, width), F32),
            pltpu.VMEM((3, width), F32),
            pltpu.VMEM((3, heads, HEAD_DIM, 2 * count), BF16),
            pltpu.VMEM((heads, HEAD_DIM, 2 * count), F32),
            pltpu.VMEM((count, width), BF16),
            pltpu.VMEM((count, width), BF16),
            pltpu.VMEM((count, width), F32),
            pltpu.VMEM((count, width), F32),
            blocks,
            blocks,
            blocks,
            pltpu.VMEM((3, depth, heads, HEAD_DIM, 2 * pos), BF16),
            pltpu.VMEM((depth, heads, HEAD_DIM, 2 * pos), F32),
            blocks,
            blocks,
            pltpu.VMEM((depth, pos, width), F32),
            blocks,
            blocks,
            dma((7,)),
            dma((group,)),
            dma((group,)),
            dma((2,)),
            dma((2,)),
            dma((2,)),
            dma((2,)),
            dma((depth,)),
            dma((depth,)),
            dma((depth,)),
            dma((depth,)),
            dma((depth,)),
            dma((depth,)),
            dma((depth,)),
            dma((depth,)),
        ],
        compiler_params=pltpu.CompilerParams(
            collective_id=0, has_side_effects=True, vmem_limit_bytes=58 * 1024 * 1024
        ),
    )(
        time_features(timestep),
        spatial_table,
        temporal_table,
        frames.reshape(count, width),
        embed_weight,
        block_weight,
        jnp.transpose(spatial_qkv, (1, 2, 0)),
        spatial_out,
        jnp.transpose(temporal_qkv, (1, 2, 0)),
        temporal_out,
    )
    return result.reshape(frames.shape)


def solution(mesh):
    return jax.shard_map(
        body,
        mesh=mesh,
        in_specs=(
            P("tp", ("clip", "seq"), None),
            P("clip"),
            P(),
            P(("seq", "tp"), None),
            P(),
            P(),
            P(None, None, "tp"),
            P("tp", None),
            P(None, None, "tp"),
            P("tp", None),
        ),
        out_specs=P("tp", ("clip", "seq"), None),
        check_vma=False,
    )
```

```python
import functools
import math

import jax
import jax.numpy as jnp
from jax import lax
from jax.experimental import pallas as pl
from jax.experimental.pallas import tpu as pltpu
from jax.sharding import PartitionSpec as P

HEAD_DIM = 72
FREQ = 256
F32 = jnp.float32
BF16 = jnp.bfloat16
MESH = pl.DeviceIdType.MESH
NT = (((1,), (1,)), ((), ()))
TN = (((0,), (0,)), ((), ()))
NN = (((1,), (0,)), ((), ()))
WAVE_REFS = 20
FACTOR = 1.0 / math.sqrt(HEAD_DIM)
FACTOR2 = FACTOR * math.log2(math.e)


def time_features(timestep):
    half = FREQ // 2
    ladder = jnp.exp(-math.log(10000.0) * jnp.arange(half, dtype=jnp.float32) / half)
    angles = timestep.astype(jnp.float32)[:, None] * ladder[None, :]
    return jnp.concatenate([jnp.cos(angles), jnp.sin(angles)], axis=-1)


def mm(a, b, dims):
    return lax.dot_general(a, b, dims, preferred_element_type=F32)


def split_rows(row):
    wide = jnp.broadcast_to(row, (8, row.shape[1]))
    first = wide.astype(BF16).astype(F32)
    rest = wide - first
    second = rest.astype(BF16).astype(F32)
    third = rest - second
    index = lax.broadcasted_iota(jnp.int32, wide.shape, 0)
    zero = jnp.zeros_like(wide)
    return jnp.where(
        index == 0, first, jnp.where(index == 1, second, jnp.where(index == 2, third, zero))
    ).astype(BF16)


def normalise(values, scale, shift):
    width = values.shape[1]
    mean = jnp.sum(values, axis=1, keepdims=True) * (1.0 / width)
    centred = values - mean
    variance = jnp.sum(centred * centred, axis=1, keepdims=True) * (1.0 / width)
    return (centred * lax.rsqrt(variance + 1e-06) * (1.0 + scale) + shift).astype(BF16)


def kernel(
    depth,
    cuts,
    feats_ref,
    table_s,
    table_t,
    frames_hbm,
    embed_hbm,
    block_hbm,
    wqs_hbm,
    wos_hbm,
    wqt_hbm,
    wot_hbm,
    out_hbm,
    frames,
    embed,
    block,
    wqs,
    wos,
    wqt,
    wot,
    theirs,
    term,
    terms,
    mods_s,
    mods_t,
    qkv,
    att,
    part_send,
    part_recv,
    own,
    middle,
    load_sem,
    term_send,
    term_recv,
    fr_send,
    fr_recv,
    part_ss,
    part_rs,
    *waves,
):
    me_s = lax.axis_index("seq")
    me_t = lax.axis_index("tp")
    peer_t = 1 - me_t
    count, width = frames.shape
    heads = qkv.shape[1]
    waves = [waves[i * WAVE_REFS : (i + 1) * WAVE_REFS] for i in range(len(cuts))]

    loads = []
    for i, (src, dst) in enumerate(
        [
            (embed_hbm, embed),
            (block_hbm, block),
            (frames_hbm, frames),
            (wqs_hbm, wqs),
            (wos_hbm, wos),
            (wqt_hbm, wqt),
            (wot_hbm, wot),
        ]
    ):
        copy = pltpu.make_async_copy(src, dst, load_sem.at[i])
        copy.start()
        loads.append(copy)

    barrier = pltpu.get_barrier_semaphore()
    peers = [(ds, dt) for ds in range(depth) for dt in range(2) if ds or dt]
    for ds, dt in peers:
        pl.semaphore_signal(
            barrier,
            inc=1,
            device_id={"seq": lax.rem(me_s + ds, depth), "tp": lax.rem(me_t + dt, 2)},
            device_id_type=MESH,
        )
    pl.semaphore_wait(barrier, len(peers))

    frame_copies = []
    for i, (r0, n) in enumerate(cuts):
        copy = pltpu.make_async_remote_copy(
            src_ref=frames_hbm.at[pl.ds(r0, n)],
            dst_ref=theirs.at[pl.ds(r0, n)],
            send_sem=fr_send.at[i],
            recv_sem=fr_recv.at[i],
            device_id={"tp": peer_t},
            device_id_type=MESH,
        )
        copy.start()
        frame_copies.append(copy)

    loads[0].wait()
    hidden = mm(split_rows(feats_ref[...]), embed[...], NN)
    hidden = hidden[0:1] + hidden[1:2] + hidden[2:3]
    hidden = hidden / (1.0 + jnp.exp(-hidden))
    share = block.shape[0]
    start = (me_s * 2 + me_t) * share
    chosen = (
        lax.broadcasted_iota(jnp.int32, (width, share), 0)
        == lax.broadcasted_iota(jnp.int32, (width, share), 1) + start
    )
    mine = mm(split_rows(hidden), chosen.astype(F32).astype(BF16), NN).astype(BF16)
    loads[1].wait()
    spread = mm(mine, block[...], NN)
    spread = spread[0:1] + spread[1:2] + spread[2:3]
    for i in range(3):
        term[i : i + 1, :] = spread[:, i * width : (i + 1) * width]
    term_copies = []
    for i, (ds, dt) in enumerate(peers):
        copy = pltpu.make_async_remote_copy(
            src_ref=term,
            dst_ref=terms.at[i],
            send_sem=term_send.at[i],
            recv_sem=term_recv.at[i],
            device_id={"seq": lax.rem(me_s + ds, depth), "tp": lax.rem(me_t + dt, 2)},
            device_id_type=MESH,
        )
        copy.start()
        term_copies.append(copy)
    total = term[...]
    for i, copy in enumerate(term_copies):
        copy.wait_recv()
        total = total + terms[i]
    mods_s[...] = table_s[...] + total
    mods_t[...] = table_t[...] + total

    def spatial_in(tokens, r0, n, c0):
        normed = jnp.concatenate(
            [
                normalise(
                    tokens[pl.ds(r0 + k, 128), :].astype(F32), mods_s[1:2, :], mods_s[0:1, :]
                )
                for k in range(0, n, 128)
            ],
            axis=0,
        )

        @pl.loop(0, 3)
        def _(j):
            rows = mm(wqs[j], normed, NT)
            qkv[j, :, :, pl.ds(c0, n)] = rows.reshape(heads, HEAD_DIM, n).astype(BF16)

    loads[2].wait()
    loads[3].wait()
    for r0, n in cuts:
        spatial_in(frames, r0, n, r0)
    for i, (r0, n) in enumerate(cuts):
        frame_copies[i].wait_recv()
        spatial_in(theirs, r0, n, count + r0)

    def attend(c0, n):
        @pl.loop(0, heads)
        def _(h):
            scores = mm(qkv[1, h], qkv[0, h, :, pl.ds(c0, n)], TN)
            peak = jnp.max(scores, axis=0, keepdims=True)
            raised = jnp.exp2((scores - peak) * FACTOR2)
            norm = jnp.sum(raised, axis=0, keepdims=True)
            att[h, :, pl.ds(c0, n)] = mm(qkv[2, h], raised.astype(BF16), NN) / norm

    def project(c0, n):
        heads_out = att[:, :, pl.ds(c0, n)].reshape(heads * HEAD_DIM, n).astype(BF16)
        return mm(heads_out, wos[...], TN)

    loads[4].wait()
    part_copies = []
    for i, (r0, n) in enumerate(cuts):
        attend(count + r0, n)
        for k in range(r0, r0 + n, 128):
            part_send[pl.ds(k, 128), :] = project(count + k, 128).astype(BF16)
        copy = pltpu.make_async_remote_copy(
            src_ref=part_send.at[pl.ds(r0, n)],
            dst_ref=part_recv.at[pl.ds(r0, n)],
            send_sem=part_ss.at[i],
            recv_sem=part_rs.at[i],
            device_id={"tp": peer_t},
            device_id_type=MESH,
        )
        copy.start()
        part_copies.append(copy)
    for r0, n in cuts:
        attend(r0, n)
    for k in range(0, count, 128):
        own[pl.ds(k, 128), :] = project(k, 128)

    def seq_copy(src, dst, send, recv, there):
        return pltpu.make_async_remote_copy(
            src_ref=src.at[there],
            dst_ref=dst.at[me_s],
            send_sem=send.at[there],
            recv_sem=recv.at[me_s],
            device_id={"seq": there},
            device_id_type=MESH,
        )

    def seq_arrival(src, dst, send, recv, there):
        return pltpu.make_async_remote_copy(
            src_ref=src.at[there],
            dst_ref=dst.at[there],
            send_sem=send.at[there],
            recv_sem=recv.at[there],
            device_id={"seq": there},
            device_id_type=MESH,
        )

    def tp_copy(src, dst, send, recv, f):
        return pltpu.make_async_remote_copy(
            src_ref=src.at[f],
            dst_ref=dst.at[f],
            send_sem=send.at[f],
            recv_sem=recv.at[f],
            device_id={"tp": peer_t},
            device_id_type=MESH,
        )

    def frame_at(d):
        return lax.rem(me_s + d, depth)

    class Wave:
        def __init__(self, i):
            self.i = i
            self.r0, self.n = cuts[i]
            self.pos = self.n // depth
            (
                self.nt,
                self.xa,
                self.xb,
                self.qkvt,
                self.attt,
                self.pb,
                self.pr,
                self.po,
                self.rs,
                self.rr,
                self.nt_send,
                self.nt_recv,
                self.fx_send,
                self.fx_recv,
                self.pb_send,
                self.pb_recv,
                self.rs_send,
                self.rs_recv,
                self.out_sem,
                self.outbuf,
            ) = waves[i]

        def middle_out(self):
            part_copies[self.i].wait_recv()
            for k in range(self.r0, self.r0 + self.n, 128):
                rows = pl.ds(k, 128)
                middle[rows, :] = frames[rows, :].astype(F32) + mods_s[2:3, :] * (
                    own[rows, :] + part_recv[rows, :].astype(F32)
                )

            @pl.loop(1, depth + 1)
            def _(d):
                b = frame_at(d)
                rows = pl.ds(pl.multiple_of(self.r0 + b * self.pos, 8), self.pos)
                self.nt[b] = normalise(middle[rows, :], mods_t[1:2, :], mods_t[0:1, :])

                @pl.when(d < depth)
                def _():
                    seq_copy(self.nt, self.xa, self.nt_send, self.nt_recv, b).start()

            self.xa[me_s] = self.nt[me_s]
            tp_copy(self.xa, self.xb, self.fx_send, self.fx_recv, me_s).start()

        def forward(self, d):
            f = frame_at(d)
            seq_arrival(self.nt, self.xa, self.nt_send, self.nt_recv, f).wait_recv()
            tp_copy(self.xa, self.xb, self.fx_send, self.fx_recv, f).start()

        def batches(self):
            size = min(depth, max(1, 256 // (2 * self.pos)))
            return [range(d, min(d + size, depth)) for d in range(0, depth, size)]

        def project_in(self, batch):
            parts = []
            for d in batch:
                f = frame_at(d)
                tp_copy(self.xa, self.xb, self.fx_send, self.fx_recv, f).wait_recv()
                parts += [self.xa[f], self.xb[f]]
            if self.pos % 16:
                parts = [part.astype(F32) for part in parts]
            tokens = jnp.concatenate(parts, axis=0).astype(BF16)
            span = 2 * self.pos
            for j in range(3):
                rows = mm(wqt[j], tokens, NT).reshape(heads, HEAD_DIM, -1)
                for k, d in enumerate(batch):
                    self.qkvt[j, frame_at(d)] = rows[:, :, k * span : (k + 1) * span].astype(BF16)

        def attend(self, d):
            f = frame_at(d)
            scores = []
            for g in range(depth):
                scores.append([])
            for h in range(heads):
                query = self.qkvt[0, f, h].astype(F32)
                for g in range(depth):
                    key = self.qkvt[1, g, h].astype(F32)
                    scores[g].append(jnp.sum(query * key, axis=0, keepdims=True))
            scores = [jnp.concatenate(rows, axis=0) * FACTOR for rows in scores]
            peak = functools.reduce(jnp.maximum, scores)
            raised = [jnp.exp(s - peak) for s in scores]
            norm = functools.reduce(jnp.add, raised)
            weights = [(r / norm).astype(BF16).astype(F32) for r in raised]
            for h in range(heads):
                result = None
                for g in range(depth):
                    piece = weights[g][h : h + 1, :] * self.qkvt[2, g, h].astype(F32)
                    result = piece if result is None else result + piece
                self.attt[h] = result
            flat = self.attt[...].reshape(heads * HEAD_DIM, 2 * self.pos).astype(BF16)
            projected = mm(flat, wot[...], TN)
            self.pb[f] = projected[self.pos :].astype(BF16)
            tp_copy(self.pb, self.pr, self.pb_send, self.pb_recv, f).start()
            self.po[f] = projected[: self.pos]

        def send_back(self, d):
            f = frame_at(d)
            tp_copy(self.pb, self.pr, self.pb_send, self.pb_recv, f).wait_recv()
            self.rs[f] = (self.po[f] + self.pr[f].astype(F32)).astype(BF16)

            @pl.when(f != me_s)
            def _():
                seq_copy(self.rs, self.rr, self.rs_send, self.rs_recv, f).start()

        def out_copy(self, b):
            return pltpu.make_async_copy(
                self.outbuf.at[b],
                out_hbm.at[pl.ds(self.r0 + b * self.pos, self.pos), 0, :],
                self.out_sem.at[b],
            )

        def finish(self, b, back):
            rows = pl.ds(pl.multiple_of(self.r0 + b * self.pos, 8), self.pos)
            self.outbuf[b] = middle[rows, :] + mods_t[2:3, :] * back[b].astype(F32)
            self.out_copy(b).start()

        def finish_all(self):
            self.finish(me_s, self.rs)

            @pl.loop(1, depth)
            def _(d):
                b = frame_at(d)
                seq_arrival(self.rs, self.rr, self.rs_send, self.rs_recv, b).wait_recv()
                self.finish(b, self.rr)

        def drain(self):
            @pl.loop(0, depth)
            def _(f):
                tp_copy(self.xa, self.xb, self.fx_send, self.fx_recv, f).wait_send()
                tp_copy(self.pb, self.pr, self.pb_send, self.pb_recv, f).wait_send()
                self.out_copy(f).wait()

                @pl.when(f != me_s)
                def _():
                    seq_copy(self.nt, self.xa, self.nt_send, self.nt_recv, f).wait_send()
                    seq_copy(self.rs, self.rr, self.rs_send, self.rs_recv, f).wait_send()

    steps = [Wave(i) for i in range(len(cuts))]
    for wave in steps:
        wave.middle_out()
    loads[5].wait()
    loads[6].wait()

    before = None
    for wave in steps:
        for batch in wave.batches():
            for d in batch:
                if d:
                    wave.forward(d)
            if before is not None:
                for d in batch:
                    before.send_back((d + 1) % depth)
            wave.project_in(batch)

        @pl.loop(0, depth)
        def _(d):
            wave.attend(d + 1)

        before = wave

    @pl.loop(0, depth)
    def _(d):
        before.send_back(d + 1)

    for wave in steps:
        wave.finish_all()

    for copy in frame_copies + term_copies + part_copies:
        copy.wait_send()
    for wave in steps:
        wave.drain()


def wave_scratch(depth, pos, width, heads):
    dma = pltpu.SemaphoreType.DMA
    blocks = pltpu.VMEM((depth, pos, width), BF16)
    return [
        blocks,
        blocks,
        blocks,
        pltpu.VMEM((3, depth, heads, HEAD_DIM, 2 * pos), BF16),
        pltpu.VMEM((heads, HEAD_DIM, 2 * pos), F32),
        blocks,
        blocks,
        pltpu.VMEM((depth, pos, width), F32),
        blocks,
        blocks,
        dma((depth,)),
        dma((depth,)),
        dma((depth,)),
        dma((depth,)),
        dma((depth,)),
        dma((depth,)),
        dma((depth,)),
        dma((depth,)),
        dma((depth,)),
        pltpu.VMEM((depth, pos, width), F32),
    ]


def body(
    frames,
    timestep,
    embed_weight,
    block_weight,
    spatial_table,
    temporal_table,
    spatial_qkv,
    spatial_out,
    temporal_qkv,
    temporal_out,
):
    depth = lax.axis_size("seq")
    count, _, width = frames.shape
    local = spatial_out.shape[0]
    heads = local // HEAD_DIM
    cuts = [(0, 256), (256, count - 256)] if count == 384 else [(0, count)]
    waves = []
    for _, rows in cuts:
        waves += wave_scratch(depth, rows // depth, width, heads)
    group = 2 * depth - 1
    vmem = pl.BlockSpec(memory_space=pltpu.VMEM)
    hbm = pl.BlockSpec(memory_space=pl.ANY)
    dma = pltpu.SemaphoreType.DMA
    result = pl.pallas_call(
        functools.partial(kernel, depth, cuts),
        out_shape=jax.ShapeDtypeStruct((count, 1, width), F32),
        in_specs=[vmem] * 3 + [hbm] * 7,
        out_specs=hbm,
        scratch_shapes=[
            pltpu.VMEM((count, width), BF16),
            pltpu.VMEM(embed_weight.shape, BF16),
            pltpu.VMEM(block_weight.shape, BF16),
            pltpu.VMEM((3, local, width), BF16),
            pltpu.VMEM((local, width), BF16),
            pltpu.VMEM((3, local, width), BF16),
            pltpu.VMEM((local, width), BF16),
            pltpu.VMEM((count, width), BF16),
            pltpu.VMEM((3, width), F32),
            pltpu.VMEM((group, 3, width), F32),
            pltpu.VMEM((3, width), F32),
            pltpu.VMEM((3, width), F32),
            pltpu.VMEM((3, heads, HEAD_DIM, 2 * count), BF16),
            pltpu.VMEM((heads, HEAD_DIM, 2 * count), F32),
            pltpu.VMEM((count, width), BF16),
            pltpu.VMEM((count, width), BF16),
            pltpu.VMEM((count, width), F32),
            pltpu.VMEM((count, width), F32),
            dma((7,)),
            dma((group,)),
            dma((group,)),
            dma((2,)),
            dma((2,)),
            dma((2,)),
            dma((2,)),
        ]
        + waves,
        compiler_params=pltpu.CompilerParams(
            collective_id=0, has_side_effects=True, vmem_limit_bytes=58 * 1024 * 1024
        ),
    )(
        time_features(timestep),
        spatial_table,
        temporal_table,
        frames.reshape(count, width),
        embed_weight,
        block_weight,
        jnp.transpose(spatial_qkv, (1, 2, 0)),
        spatial_out,
        jnp.transpose(temporal_qkv, (1, 2, 0)),
        temporal_out,
    )
    return result


def solution(mesh):
    return jax.shard_map(
        body,
        mesh=mesh,
        in_specs=(
            P("tp", ("clip", "seq"), None),
            P("clip"),
            P(),
            P(("seq", "tp"), None),
            P(),
            P(),
            P(None, None, "tp"),
            P("tp", None),
            P(None, None, "tp"),
            P("tp", None),
        ),
        out_specs=P("tp", ("clip", "seq"), None),
        check_vma=False,
    )
```

```python
import functools
import math

import jax
import jax.numpy as jnp
from jax import lax
from jax.experimental import pallas as pl
from jax.experimental.pallas import tpu as pltpu
from jax.sharding import PartitionSpec as P

HEAD_DIM = 72
FREQ = 256
F32 = jnp.float32
BF16 = jnp.bfloat16
MESH = pl.DeviceIdType.MESH
NT = (((1,), (1,)), ((), ()))
TN = (((0,), (0,)), ((), ()))
NN = (((1,), (0,)), ((), ()))
WAVE_REFS = 18
FACTOR = 1.0 / math.sqrt(HEAD_DIM)
FACTOR2 = FACTOR * math.log2(math.e)


def time_features(timestep):
    half = FREQ // 2
    ladder = jnp.exp(-math.log(10000.0) * jnp.arange(half, dtype=jnp.float32) / half)
    angles = timestep.astype(jnp.float32)[:, None] * ladder[None, :]
    return jnp.concatenate([jnp.cos(angles), jnp.sin(angles)], axis=-1)


def mm(a, b, dims):
    return lax.dot_general(a, b, dims, preferred_element_type=F32)


def split_rows(row):
    wide = jnp.broadcast_to(row, (8, row.shape[1]))
    first = wide.astype(BF16).astype(F32)
    rest = wide - first
    second = rest.astype(BF16).astype(F32)
    third = rest - second
    index = lax.broadcasted_iota(jnp.int32, wide.shape, 0)
    zero = jnp.zeros_like(wide)
    return jnp.where(
        index == 0, first, jnp.where(index == 1, second, jnp.where(index == 2, third, zero))
    ).astype(BF16)


def normalise(values, scale, shift):
    width = values.shape[1]
    mean = jnp.sum(values, axis=1, keepdims=True) * (1.0 / width)
    centred = values - mean
    variance = jnp.sum(centred * centred, axis=1, keepdims=True) * (1.0 / width)
    return (centred * lax.rsqrt(variance + 1e-06) * (1.0 + scale) + shift).astype(BF16)


def kernel(
    depth,
    cuts,
    feats_ref,
    table_s,
    table_t,
    frames_hbm,
    embed_hbm,
    block_hbm,
    wqs_hbm,
    wos_hbm,
    wqt_hbm,
    wot_hbm,
    out_ref,
    frames,
    embed,
    block,
    wqs,
    wos,
    wqt,
    wot,
    theirs,
    term,
    terms,
    mods_s,
    mods_t,
    qkv,
    att,
    part_send,
    part_recv,
    own,
    middle,
    load_sem,
    term_send,
    term_recv,
    fr_send,
    fr_recv,
    part_ss,
    part_rs,
    keys,
    wot_other,
    wx_send,
    wx_recv,
    *waves,
):
    me_s = lax.axis_index("seq")
    me_t = lax.axis_index("tp")
    peer_t = 1 - me_t
    count, width = frames.shape
    heads = qkv.shape[1]
    waves = [waves[i * WAVE_REFS : (i + 1) * WAVE_REFS] for i in range(len(cuts))]

    loads = []
    for i, (src, dst) in enumerate(
        [
            (embed_hbm, embed),
            (block_hbm, block),
            (frames_hbm, frames),
            (wqs_hbm, wqs),
            (wos_hbm, wos),
            (wqt_hbm, wqt),
            (wot_hbm, wot),
        ]
    ):
        copy = pltpu.make_async_copy(src, dst, load_sem.at[i])
        copy.start()
        loads.append(copy)

    barrier = pltpu.get_barrier_semaphore()
    peers = [(ds, dt) for ds in range(depth) for dt in range(2) if ds or dt]
    for ds, dt in peers:
        pl.semaphore_signal(
            barrier,
            inc=1,
            device_id={"seq": lax.rem(me_s + ds, depth), "tp": lax.rem(me_t + dt, 2)},
            device_id_type=MESH,
        )
    parts = wx_send.shape[0]
    me_c = lax.axis_index("clip")
    piece = lax.rem(me_c, parts)
    for k in range(1, parts):
        pl.semaphore_signal(
            barrier,
            inc=1,
            device_id={"clip": me_c - piece + lax.rem(piece + k, parts)},
            device_id_type=MESH,
        )
    pl.semaphore_wait(barrier, len(peers) + parts - 1)

    frame_copies = []
    for i, (r0, n) in enumerate(cuts):
        copy = pltpu.make_async_remote_copy(
            src_ref=frames_hbm.at[pl.ds(r0, n)],
            dst_ref=theirs.at[pl.ds(r0, n)],
            send_sem=fr_send.at[i],
            recv_sem=fr_recv.at[i],
            device_id={"tp": peer_t},
            device_id_type=MESH,
        )
        copy.start()
        frame_copies.append(copy)

    loads[0].wait()
    hidden = mm(split_rows(feats_ref[...]), embed[...], NN)
    hidden = hidden[0:1] + hidden[1:2] + hidden[2:3]
    hidden = hidden / (1.0 + jnp.exp(-hidden))
    share = block.shape[0]
    start = (me_s * 2 + me_t) * share
    chosen = (
        lax.broadcasted_iota(jnp.int32, (width, share), 0)
        == lax.broadcasted_iota(jnp.int32, (width, share), 1) + start
    )
    mine = mm(split_rows(hidden), chosen.astype(F32).astype(BF16), NN).astype(BF16)
    loads[1].wait()
    spread = mm(mine, block[...], NN)
    spread = spread[0:1] + spread[1:2] + spread[2:3]
    for i in range(3):
        term[i : i + 1, :] = spread[:, i * width : (i + 1) * width]
    term_copies = []
    for i, (ds, dt) in enumerate(peers):
        copy = pltpu.make_async_remote_copy(
            src_ref=term,
            dst_ref=terms.at[i],
            send_sem=term_send.at[i],
            recv_sem=term_recv.at[i],
            device_id={"seq": lax.rem(me_s + ds, depth), "tp": lax.rem(me_t + dt, 2)},
            device_id_type=MESH,
        )
        copy.start()
        term_copies.append(copy)
    total = term[...]
    for i, copy in enumerate(term_copies):
        copy.wait_recv()
        total = total + terms[i]
    mods_s[...] = table_s[...] + total
    mods_t[...] = table_t[...] + total

    def spatial_in(tokens, r0, n, c0):
        normed = jnp.concatenate(
            [
                normalise(
                    tokens[pl.ds(r0 + k, 128), :].astype(F32), mods_s[1:2, :], mods_s[0:1, :]
                )
                for k in range(0, n, 128)
            ],
            axis=0,
        )

        @pl.loop(0, 3)
        def _(j):
            rows = mm(wqs[j], normed, NT).reshape(heads, HEAD_DIM, n)
            qkv[j, :, :, pl.ds(c0, n)] = rows.astype(BF16)

            @pl.when(j == 1)
            def _():
                for h in range(heads):
                    keys[h, pl.ds(c0, n), :] = rows[h].T.astype(BF16)

    loads[2].wait()
    loads[3].wait()
    for r0, n in cuts:
        spatial_in(frames, r0, n, r0)
    for i, (r0, n) in enumerate(cuts):
        frame_copies[i].wait_recv()
        if i == len(cuts) - 1:
            slice_rows = wot.shape[0] // parts
            wot_rows = pl.ds(pl.multiple_of(piece * slice_rows, 16), slice_rows)
            wot_fetch = pltpu.make_async_remote_copy(
                src_ref=wot_hbm.at[wot_rows],
                dst_ref=wot_other.at[wot_rows],
                send_sem=wx_send.at[0],
                recv_sem=wx_recv.at[0],
                device_id={"tp": peer_t},
                device_id_type=MESH,
            )
            wot_fetch.start()
        spatial_in(theirs, r0, n, count + r0)

    def attend(c0, n):
        @pl.loop(0, heads)
        def _(h):
            scores = mm(keys[h], qkv[0, h, :, pl.ds(c0, n)], NN)
            peak = jnp.max(scores, axis=0, keepdims=True)
            raised = jnp.exp2((scores - peak) * FACTOR2)
            norm = jnp.sum(raised, axis=0, keepdims=True)
            att[h, :, pl.ds(c0, n)] = mm(qkv[2, h], raised.astype(BF16), NN) / norm

    def project(c0, n):
        heads_out = att[:, :, pl.ds(c0, n)].reshape(heads * HEAD_DIM, n).astype(BF16)
        return mm(heads_out, wos[...], TN)

    loads[4].wait()
    part_copies = []
    for i, (r0, n) in enumerate(cuts):
        attend(count + r0, n)
        for k in range(r0, r0 + n, 128):
            part_send[pl.ds(k, 128), :] = project(count + k, 128).astype(BF16)
        copy = pltpu.make_async_remote_copy(
            src_ref=part_send.at[pl.ds(r0, n)],
            dst_ref=part_recv.at[pl.ds(r0, n)],
            send_sem=part_ss.at[i],
            recv_sem=part_rs.at[i],
            device_id={"tp": peer_t},
            device_id_type=MESH,
        )
        copy.start()
        part_copies.append(copy)
    wot_fetch.wait_recv()
    wot_copies = []
    for k in range(1, parts):
        copy = pltpu.make_async_remote_copy(
            src_ref=wot_other.at[wot_rows],
            dst_ref=wot_other.at[wot_rows],
            send_sem=wx_send.at[k],
            recv_sem=wx_recv.at[k],
            device_id={"clip": me_c - piece + lax.rem(piece + k, parts)},
            device_id_type=MESH,
        )
        copy.start()
        wot_copies.append(copy)
    for r0, n in cuts:
        attend(r0, n)
    for k in range(0, count, 128):
        own[pl.ds(k, 128), :] = project(k, 128)

    def seq_copy(src, dst, send, recv, there):
        return pltpu.make_async_remote_copy(
            src_ref=src.at[there],
            dst_ref=dst.at[me_s],
            send_sem=send.at[there],
            recv_sem=recv.at[me_s],
            device_id={"seq": there},
            device_id_type=MESH,
        )

    def seq_arrival(src, dst, send, recv, there):
        return pltpu.make_async_remote_copy(
            src_ref=src.at[there],
            dst_ref=dst.at[there],
            send_sem=send.at[there],
            recv_sem=recv.at[there],
            device_id={"seq": there},
            device_id_type=MESH,
        )

    def tp_copy(src, dst, send, recv, f):
        return pltpu.make_async_remote_copy(
            src_ref=src.at[f],
            dst_ref=dst.at[f],
            send_sem=send.at[f],
            recv_sem=recv.at[f],
            device_id={"tp": peer_t},
            device_id_type=MESH,
        )

    def frame_at(d):
        return lax.rem(me_s + d, depth)

    class Wave:
        def __init__(self, i):
            self.i = i
            self.r0, self.n = cuts[i]
            self.pos = self.n // depth
            (
                self.nt,
                self.xa,
                self.xb,
                self.qkvt,
                self.attt,
                self.pb,
                self.pr,
                self.po,
                self.rs,
                self.rr,
                self.nt_send,
                self.nt_recv,
                self.fx_send,
                self.fx_recv,
                self.pb_send,
                self.pb_recv,
                self.rs_send,
                self.rs_recv,
            ) = waves[i]

        def middle_out(self):
            part_copies[self.i].wait_recv()
            for k in range(self.r0, self.r0 + self.n, 128):
                rows = pl.ds(k, 128)
                middle[rows, :] = frames[rows, :].astype(F32) + mods_s[2:3, :] * (
                    own[rows, :] + part_recv[rows, :].astype(F32)
                )

            @pl.loop(1, depth + 1)
            def _(d):
                b = frame_at(d)
                rows = pl.ds(pl.multiple_of(self.r0 + b * self.pos, 8), self.pos)
                self.nt[b] = normalise(middle[rows, :], mods_t[1:2, :], mods_t[0:1, :])

                @pl.when(d < depth)
                def _():
                    seq_copy(self.nt, self.xa, self.nt_send, self.nt_recv, b).start()

            self.xa[me_s] = self.nt[me_s]
            tp_copy(self.xa, self.xb, self.fx_send, self.fx_recv, me_s).start()

        def forward(self, d):
            f = frame_at(d)
            seq_arrival(self.nt, self.xa, self.nt_send, self.nt_recv, f).wait_recv()
            tp_copy(self.xa, self.xb, self.fx_send, self.fx_recv, f).start()

        def batches(self):
            size = min(depth, max(1, 256 // (2 * self.pos)))
            return [range(d, min(d + size, depth)) for d in range(0, depth, size)]

        def project_in(self, batch):
            parts = []
            for d in batch:
                f = frame_at(d)
                tp_copy(self.xa, self.xb, self.fx_send, self.fx_recv, f).wait_recv()
                parts += [self.xa[f], self.xb[f]]
            if self.pos % 16:
                parts = [part.astype(F32) for part in parts]
            tokens = jnp.concatenate(parts, axis=0).astype(BF16)
            span = 2 * self.pos
            for j in range(3):
                rows = mm(wqt[j], tokens, NT).reshape(heads, HEAD_DIM, -1)
                for k, d in enumerate(batch):
                    self.qkvt[j, frame_at(d)] = rows[:, :, k * span : (k + 1) * span].astype(BF16)

        def attend(self, d):
            f = frame_at(d)
            scores = []
            for g in range(depth):
                scores.append([])
            for h in range(heads):
                query = self.qkvt[0, f, h].astype(F32)
                for g in range(depth):
                    key = self.qkvt[1, g, h].astype(F32)
                    scores[g].append(jnp.sum(query * key, axis=0, keepdims=True))
            scores = [jnp.concatenate(rows, axis=0) * FACTOR for rows in scores]
            peak = functools.reduce(jnp.maximum, scores)
            raised = [jnp.exp(s - peak) for s in scores]
            norm = functools.reduce(jnp.add, raised)
            weights = [(r / norm).astype(BF16).astype(F32) for r in raised]
            for h in range(heads):
                result = None
                for g in range(depth):
                    piece = weights[g][h : h + 1, :] * self.qkvt[2, g, h].astype(F32)
                    result = piece if result is None else result + piece
                self.attt[h] = result
            flat = self.attt[...].reshape(heads * HEAD_DIM, 2 * self.pos).T
            self.pb[f] = flat[self.pos :].astype(BF16)
            tp_copy(self.pb, self.pr, self.pb_send, self.pb_recv, f).start()
            self.po[f] = flat[: self.pos].astype(BF16)

        def send_back(self, d):
            f = frame_at(d)
            tp_copy(self.pb, self.pr, self.pb_send, self.pb_recv, f).wait_recv()
            self.rs[f] = (
                mm(self.po[f], wot[...], NN) + mm(self.pr[f], wot_other[...], NN)
            ).astype(BF16)

            @pl.when(f != me_s)
            def _():
                seq_copy(self.rs, self.rr, self.rs_send, self.rs_recv, f).start()

        def finish(self, b, back):
            rows = pl.ds(pl.multiple_of(self.r0 + b * self.pos, 8), self.pos)
            out_ref[rows, :] = middle[rows, :] + mods_t[2:3, :] * back[b].astype(F32)

        def finish_all(self):
            self.finish(me_s, self.rs)

            @pl.loop(1, depth)
            def _(d):
                b = frame_at(d)
                seq_arrival(self.rs, self.rr, self.rs_send, self.rs_recv, b).wait_recv()
                self.finish(b, self.rr)

        def drain(self):
            @pl.loop(0, depth)
            def _(f):
                tp_copy(self.xa, self.xb, self.fx_send, self.fx_recv, f).wait_send()
                tp_copy(self.pb, self.pr, self.pb_send, self.pb_recv, f).wait_send()

                @pl.when(f != me_s)
                def _():
                    seq_copy(self.nt, self.xa, self.nt_send, self.nt_recv, f).wait_send()
                    seq_copy(self.rs, self.rr, self.rs_send, self.rs_recv, f).wait_send()

    steps = [Wave(i) for i in range(len(cuts))]
    for wave in steps:
        wave.middle_out()
    loads[5].wait()
    loads[6].wait()

    before = None
    for wave in steps:
        for batch in wave.batches():
            for d in batch:
                if d:
                    wave.forward(d)
            if before is not None:
                if batch[0] == 0:
                    for copy in wot_copies:
                        copy.wait_recv()
                for d in batch:
                    before.send_back((d + 1) % depth)
            wave.project_in(batch)

        @pl.loop(0, depth)
        def _(d):
            wave.attend(d + 1)

        before = wave

    if len(steps) == 1:
        for copy in wot_copies:
            copy.wait_recv()

    @pl.loop(0, depth)
    def _(d):
        before.send_back(d + 1)

    for wave in steps:
        wave.finish_all()

    for copy in frame_copies + term_copies + part_copies + [wot_fetch] + wot_copies:
        copy.wait_send()
    for wave in steps:
        wave.drain()


def wave_scratch(depth, pos, width, heads):
    dma = pltpu.SemaphoreType.DMA
    blocks = pltpu.VMEM((depth, pos, width), BF16)
    halves = pltpu.VMEM((depth, pos, heads * HEAD_DIM), BF16)
    return [
        blocks,
        blocks,
        blocks,
        pltpu.VMEM((3, depth, heads, HEAD_DIM, 2 * pos), BF16),
        pltpu.VMEM((heads, HEAD_DIM, 2 * pos), F32),
        halves,
        halves,
        halves,
        blocks,
        blocks,
        dma((depth,)),
        dma((depth,)),
        dma((depth,)),
        dma((depth,)),
        dma((depth,)),
        dma((depth,)),
        dma((depth,)),
        dma((depth,)),
    ]


def write_out(src, dst, sem):
    rows = src.shape[0] // 3
    copies = [
        pltpu.make_async_copy(
            src.at[pl.ds(i * rows, rows)], dst.at[pl.ds(i * rows, rows), 0, :], sem.at[i]
        )
        for i in range(3)
    ]
    for copy in copies:
        copy.start()
    for copy in copies:
        copy.wait()


def body(
    frames,
    timestep,
    embed_weight,
    block_weight,
    spatial_table,
    temporal_table,
    spatial_qkv,
    spatial_out,
    temporal_qkv,
    temporal_out,
):
    depth = lax.axis_size("seq")
    count, _, width = frames.shape
    local = spatial_out.shape[0]
    heads = local // HEAD_DIM
    cuts = [(0, 256), (256, count - 256)] if count == 384 else [(0, count)]
    parts = min(4, lax.axis_size("clip"))
    waves = []
    for _, rows in cuts:
        waves += wave_scratch(depth, rows // depth, width, heads)
    group = 2 * depth - 1
    vmem = pl.BlockSpec(memory_space=pltpu.VMEM)
    hbm = pl.BlockSpec(memory_space=pl.ANY)
    dma = pltpu.SemaphoreType.DMA
    result = pl.pallas_call(
        functools.partial(kernel, depth, cuts),
        out_shape=jax.ShapeDtypeStruct((count, width), F32),
        in_specs=[vmem] * 3 + [hbm] * 7,
        out_specs=vmem,
        scratch_shapes=[
            pltpu.VMEM((count, width), BF16),
            pltpu.VMEM(embed_weight.shape, BF16),
            pltpu.VMEM(block_weight.shape, BF16),
            pltpu.VMEM((3, local, width), BF16),
            pltpu.VMEM((local, width), BF16),
            pltpu.VMEM((3, local, width), BF16),
            pltpu.VMEM((local, width), BF16),
            pltpu.VMEM((count, width), BF16),
            pltpu.VMEM((3, width), F32),
            pltpu.VMEM((group, 3, width), F32),
            pltpu.VMEM((3, width), F32),
            pltpu.VMEM((3, width), F32),
            pltpu.VMEM((3, heads, HEAD_DIM, 2 * count), BF16),
            pltpu.VMEM((heads, HEAD_DIM, 2 * count), F32),
            pltpu.VMEM((count, width), BF16),
            pltpu.VMEM((count, width), BF16),
            pltpu.VMEM((count, width), F32),
            pltpu.VMEM((count, width), F32),
            dma((7,)),
            dma((group,)),
            dma((group,)),
            dma((2,)),
            dma((2,)),
            dma((2,)),
            dma((2,)),
            pltpu.VMEM((heads, 2 * count, HEAD_DIM), BF16),
            pltpu.VMEM((local, width), BF16),
            dma((parts,)),
            dma((parts,)),
        ]
        + waves,
        compiler_params=pltpu.CompilerParams(
            collective_id=0, has_side_effects=True, vmem_limit_bytes=58 * 1024 * 1024
        ),
    )(
        time_features(timestep),
        spatial_table,
        temporal_table,
        frames.reshape(count, width),
        embed_weight,
        block_weight,
        jnp.transpose(spatial_qkv, (1, 2, 0)),
        spatial_out,
        jnp.transpose(temporal_qkv, (1, 2, 0)),
        temporal_out,
    )
    return pl.pallas_call(
        write_out,
        out_shape=jax.ShapeDtypeStruct(frames.shape, F32),
        in_specs=[hbm],
        out_specs=hbm,
        scratch_shapes=[dma((3,))],
    )(result)


def solution(mesh):
    return jax.shard_map(
        body,
        mesh=mesh,
        in_specs=(
            P("tp", ("clip", "seq"), None),
            P("clip"),
            P(),
            P(("seq", "tp"), None),
            P(),
            P(),
            P(None, None, "tp"),
            P("tp", None),
            P(None, None, "tp"),
            P("tp", None),
        ),
        out_specs=P("tp", ("clip", "seq"), None),
        check_vma=False,
    )
```

```python
import functools
import math

import jax
import jax.numpy as jnp
from jax import lax
from jax.experimental import pallas as pl
from jax.experimental.pallas import tpu as pltpu
from jax.sharding import PartitionSpec as P

HEAD_DIM = 72
FREQ = 256
F32 = jnp.float32
BF16 = jnp.bfloat16
MESH = pl.DeviceIdType.MESH
NT = (((1,), (1,)), ((), ()))
TN = (((0,), (0,)), ((), ()))
NN = (((1,), (0,)), ((), ()))
WAVE_REFS = 18
FACTOR = 1.0 / math.sqrt(HEAD_DIM)
FACTOR2 = FACTOR * math.log2(math.e)


def time_features(timestep):
    half = FREQ // 2
    ladder = jnp.exp(-math.log(10000.0) * jnp.arange(half, dtype=jnp.float32) / half)
    angles = timestep.astype(jnp.float32)[:, None] * ladder[None, :]
    return jnp.concatenate([jnp.cos(angles), jnp.sin(angles)], axis=-1)


def mm(a, b, dims):
    return lax.dot_general(a, b, dims, preferred_element_type=F32)


def split_rows(row):
    wide = jnp.broadcast_to(row, (8, row.shape[1]))
    first = wide.astype(BF16).astype(F32)
    rest = wide - first
    second = rest.astype(BF16).astype(F32)
    third = rest - second
    index = lax.broadcasted_iota(jnp.int32, wide.shape, 0)
    zero = jnp.zeros_like(wide)
    return jnp.where(
        index == 0, first, jnp.where(index == 1, second, jnp.where(index == 2, third, zero))
    ).astype(BF16)


def normalise(values, scale, shift):
    width = values.shape[1]
    mean = jnp.sum(values, axis=1, keepdims=True) * (1.0 / width)
    centred = values - mean
    variance = jnp.sum(centred * centred, axis=1, keepdims=True) * (1.0 / width)
    return (centred * lax.rsqrt(variance + 1e-06) * (1.0 + scale) + shift).astype(BF16)


def kernel(
    depth,
    cuts,
    feats_ref,
    table_s,
    table_t,
    frames_hbm,
    embed_hbm,
    block_hbm,
    wqs_hbm,
    wos_hbm,
    wqt_hbm,
    wot_hbm,
    out_ref,
    frames,
    embed,
    block,
    wqs,
    wos,
    wqt,
    wot,
    theirs,
    term,
    terms,
    mods_s,
    mods_t,
    qkv,
    att,
    part_send,
    part_recv,
    own,
    middle,
    load_sem,
    term_send,
    term_recv,
    fr_send,
    fr_recv,
    part_ss,
    part_rs,
    keys,
    wot_other,
    wx_send,
    wx_recv,
    peaks,
    norms,
    *waves,
):
    me_s = lax.axis_index("seq")
    me_t = lax.axis_index("tp")
    peer_t = 1 - me_t
    count, width = frames.shape
    heads = qkv.shape[1]
    waves = [waves[i * WAVE_REFS : (i + 1) * WAVE_REFS] for i in range(len(cuts))]

    loads = []
    for i, (src, dst) in enumerate(
        [
            (embed_hbm, embed),
            (block_hbm, block),
            (frames_hbm, frames),
            (wqs_hbm, wqs),
            (wos_hbm, wos),
            (wqt_hbm, wqt),
            (wot_hbm, wot),
        ]
    ):
        copy = pltpu.make_async_copy(src, dst, load_sem.at[i])
        copy.start()
        loads.append(copy)

    barrier = pltpu.get_barrier_semaphore()
    peers = [(ds, dt) for ds in range(depth) for dt in range(2) if ds or dt]
    for ds, dt in peers:
        pl.semaphore_signal(
            barrier,
            inc=1,
            device_id={"seq": lax.rem(me_s + ds, depth), "tp": lax.rem(me_t + dt, 2)},
            device_id_type=MESH,
        )
    parts = wx_send.shape[0]
    me_c = lax.axis_index("clip")
    piece = lax.rem(me_c, parts)
    for k in range(1, parts):
        pl.semaphore_signal(
            barrier,
            inc=1,
            device_id={"clip": me_c - piece + lax.rem(piece + k, parts)},
            device_id_type=MESH,
        )
    pl.semaphore_wait(barrier, len(peers) + parts - 1)

    frame_copies = []
    for i, (r0, n) in enumerate(cuts):
        copy = pltpu.make_async_remote_copy(
            src_ref=frames_hbm.at[pl.ds(r0, n)],
            dst_ref=theirs.at[pl.ds(r0, n)],
            send_sem=fr_send.at[i],
            recv_sem=fr_recv.at[i],
            device_id={"tp": peer_t},
            device_id_type=MESH,
        )
        copy.start()
        frame_copies.append(copy)

    loads[0].wait()
    hidden = mm(split_rows(feats_ref[...]), embed[...], NN)
    hidden = hidden[0:1] + hidden[1:2] + hidden[2:3]
    hidden = hidden / (1.0 + jnp.exp(-hidden))
    share = block.shape[0]
    start = (me_s * 2 + me_t) * share
    chosen = (
        lax.broadcasted_iota(jnp.int32, (width, share), 0)
        == lax.broadcasted_iota(jnp.int32, (width, share), 1) + start
    )
    mine = mm(split_rows(hidden), chosen.astype(F32).astype(BF16), NN).astype(BF16)
    loads[1].wait()
    spread = mm(mine, block[...], NN)
    spread = spread[0:1] + spread[1:2] + spread[2:3]
    for i in range(3):
        term[i : i + 1, :] = spread[:, i * width : (i + 1) * width]
    term_copies = []
    for i, (ds, dt) in enumerate(peers):
        copy = pltpu.make_async_remote_copy(
            src_ref=term,
            dst_ref=terms.at[i],
            send_sem=term_send.at[i],
            recv_sem=term_recv.at[i],
            device_id={"seq": lax.rem(me_s + ds, depth), "tp": lax.rem(me_t + dt, 2)},
            device_id_type=MESH,
        )
        copy.start()
        term_copies.append(copy)
    total = term[...]
    for i, copy in enumerate(term_copies):
        copy.wait_recv()
        total = total + terms[i]
    mods_s[...] = table_s[...] + total
    mods_t[...] = table_t[...] + total

    def spatial_in(tokens, r0, n, c0):
        normed = jnp.concatenate(
            [
                normalise(
                    tokens[pl.ds(r0 + k, 128), :].astype(F32), mods_s[1:2, :], mods_s[0:1, :]
                )
                for k in range(0, n, 128)
            ],
            axis=0,
        )

        @pl.loop(0, 3)
        def _(j):
            rows = mm(wqs[j], normed, NT).reshape(heads, HEAD_DIM, n)
            qkv[j, :, :, pl.ds(c0, n)] = rows.astype(BF16)

            @pl.when(j == 1)
            def _():
                for h in range(heads):
                    keys[h, pl.ds(c0, n), :] = rows[h].T.astype(BF16)

    def attend(c0, n, k0, extent, first, last):
        here = pl.ds(c0, n)

        @pl.loop(0, heads)
        def _(h):
            scores = mm(keys[h, pl.ds(k0, extent), :], qkv[0, h, :, here], NN)
            peak = jnp.max(scores, axis=0, keepdims=True)
            if not first:
                before = peaks[h, :, here]
                peak = jnp.maximum(peak, before)
                shrink = jnp.exp2((before - peak) * FACTOR2)
            raised = jnp.exp2((scores - peak) * FACTOR2)
            norm = jnp.sum(raised, axis=0, keepdims=True)
            result = mm(qkv[2, h, :, pl.ds(k0, extent)], raised.astype(BF16), NN)
            if not first:
                norm = norm + norms[h, :, here] * shrink
                result = result + att[h, :, here] * shrink
            if last:
                att[h, :, here] = result / norm
            else:
                peaks[h, :, here] = peak
                norms[h, :, here] = norm
                att[h, :, here] = result

    loads[2].wait()
    loads[3].wait()
    for r0, n in cuts:
        spatial_in(frames, r0, n, r0)
    for r0, n in cuts:
        attend(r0, n, 0, count, True, False)
    for i, (r0, n) in enumerate(cuts):
        frame_copies[i].wait_recv()
        if i == len(cuts) - 1:
            slice_rows = wot.shape[0] // parts
            wot_rows = pl.ds(pl.multiple_of(piece * slice_rows, 16), slice_rows)
            wot_fetch = pltpu.make_async_remote_copy(
                src_ref=wot_hbm.at[wot_rows],
                dst_ref=wot_other.at[wot_rows],
                send_sem=wx_send.at[0],
                recv_sem=wx_recv.at[0],
                device_id={"tp": peer_t},
                device_id_type=MESH,
            )
            wot_fetch.start()
        spatial_in(theirs, r0, n, count + r0)
        if i < len(cuts) - 1:
            attend(count + r0, n, 0, count + r0 + n, True, False)

    def project(c0, n):
        heads_out = att[:, :, pl.ds(c0, n)].reshape(heads * HEAD_DIM, n).astype(BF16)
        return mm(heads_out, wos[...], TN)

    loads[4].wait()
    part_copies = []
    for i, (r0, n) in enumerate(cuts):
        if i < len(cuts) - 1:
            attend(count + r0, n, count + r0 + n, count - r0 - n, False, True)
        else:
            attend(count + r0, n, 0, 2 * count, True, True)
        for k in range(r0, r0 + n, 128):
            part_send[pl.ds(k, 128), :] = project(count + k, 128).astype(BF16)
        copy = pltpu.make_async_remote_copy(
            src_ref=part_send.at[pl.ds(r0, n)],
            dst_ref=part_recv.at[pl.ds(r0, n)],
            send_sem=part_ss.at[i],
            recv_sem=part_rs.at[i],
            device_id={"tp": peer_t},
            device_id_type=MESH,
        )
        copy.start()
        part_copies.append(copy)
    wot_fetch.wait_recv()
    wot_copies = []
    for k in range(1, parts):
        copy = pltpu.make_async_remote_copy(
            src_ref=wot_other.at[wot_rows],
            dst_ref=wot_other.at[wot_rows],
            send_sem=wx_send.at[k],
            recv_sem=wx_recv.at[k],
            device_id={"clip": me_c - piece + lax.rem(piece + k, parts)},
            device_id_type=MESH,
        )
        copy.start()
        wot_copies.append(copy)
    for r0, n in cuts:
        attend(r0, n, count, count, False, True)
    for k in range(0, count, 128):
        own[pl.ds(k, 128), :] = project(k, 128)

    def seq_copy(src, dst, send, recv, there):
        return pltpu.make_async_remote_copy(
            src_ref=src.at[there],
            dst_ref=dst.at[me_s],
            send_sem=send.at[there],
            recv_sem=recv.at[me_s],
            device_id={"seq": there},
            device_id_type=MESH,
        )

    def seq_arrival(src, dst, send, recv, there):
        return pltpu.make_async_remote_copy(
            src_ref=src.at[there],
            dst_ref=dst.at[there],
            send_sem=send.at[there],
            recv_sem=recv.at[there],
            device_id={"seq": there},
            device_id_type=MESH,
        )

    def tp_copy(src, dst, send, recv, f):
        return pltpu.make_async_remote_copy(
            src_ref=src.at[f],
            dst_ref=dst.at[f],
            send_sem=send.at[f],
            recv_sem=recv.at[f],
            device_id={"tp": peer_t},
            device_id_type=MESH,
        )

    def frame_at(d):
        return lax.rem(me_s + d, depth)

    class Wave:
        def __init__(self, i):
            self.i = i
            self.r0, self.n = cuts[i]
            self.pos = self.n // depth
            (
                self.nt,
                self.xa,
                self.xb,
                self.qkvt,
                self.attt,
                self.pb,
                self.pr,
                self.po,
                self.rs,
                self.rr,
                self.nt_send,
                self.nt_recv,
                self.fx_send,
                self.fx_recv,
                self.pb_send,
                self.pb_recv,
                self.rs_send,
                self.rs_recv,
            ) = waves[i]

        def middle_out(self):
            part_copies[self.i].wait_recv()
            for k in range(self.r0, self.r0 + self.n, 128):
                rows = pl.ds(k, 128)
                middle[rows, :] = frames[rows, :].astype(F32) + mods_s[2:3, :] * (
                    own[rows, :] + part_recv[rows, :].astype(F32)
                )

            @pl.loop(1, depth + 1)
            def _(d):
                b = frame_at(d)
                rows = pl.ds(pl.multiple_of(self.r0 + b * self.pos, 8), self.pos)
                self.nt[b] = normalise(middle[rows, :], mods_t[1:2, :], mods_t[0:1, :])

                @pl.when(d < depth)
                def _():
                    seq_copy(self.nt, self.xa, self.nt_send, self.nt_recv, b).start()

            self.xa[me_s] = self.nt[me_s]
            tp_copy(self.xa, self.xb, self.fx_send, self.fx_recv, me_s).start()

        def forward(self, d):
            f = frame_at(d)
            seq_arrival(self.nt, self.xa, self.nt_send, self.nt_recv, f).wait_recv()
            tp_copy(self.xa, self.xb, self.fx_send, self.fx_recv, f).start()

        def batches(self):
            size = min(depth, max(1, 256 // (2 * self.pos)))
            return [range(d, min(d + size, depth)) for d in range(0, depth, size)]

        def project_in(self, batch):
            parts = []
            for d in batch:
                f = frame_at(d)
                tp_copy(self.xa, self.xb, self.fx_send, self.fx_recv, f).wait_recv()
                parts += [self.xa[f], self.xb[f]]
            if self.pos % 16:
                parts = [part.astype(F32) for part in parts]
            tokens = jnp.concatenate(parts, axis=0).astype(BF16)
            span = 2 * self.pos
            for j in range(3):
                rows = mm(wqt[j], tokens, NT).reshape(heads, HEAD_DIM, -1)
                for k, d in enumerate(batch):
                    self.qkvt[j, frame_at(d)] = rows[:, :, k * span : (k + 1) * span].astype(BF16)

        def attend(self, d):
            f = frame_at(d)
            scores = []
            for g in range(depth):
                scores.append([])
            for h in range(heads):
                query = self.qkvt[0, f, h].astype(F32)
                for g in range(depth):
                    key = self.qkvt[1, g, h].astype(F32)
                    scores[g].append(jnp.sum(query * key, axis=0, keepdims=True))
            scores = [jnp.concatenate(rows, axis=0) * FACTOR for rows in scores]
            peak = functools.reduce(jnp.maximum, scores)
            raised = [jnp.exp(s - peak) for s in scores]
            norm = functools.reduce(jnp.add, raised)
            weights = [(r / norm).astype(BF16).astype(F32) for r in raised]
            for h in range(heads):
                result = None
                for g in range(depth):
                    piece = weights[g][h : h + 1, :] * self.qkvt[2, g, h].astype(F32)
                    result = piece if result is None else result + piece
                self.attt[h] = result
            flat = self.attt[...].reshape(heads * HEAD_DIM, 2 * self.pos).T
            self.pb[f] = flat[self.pos :].astype(BF16)
            tp_copy(self.pb, self.pr, self.pb_send, self.pb_recv, f).start()
            self.po[f] = flat[: self.pos].astype(BF16)

        def send_back(self, d):
            f = frame_at(d)
            tp_copy(self.pb, self.pr, self.pb_send, self.pb_recv, f).wait_recv()
            self.rs[f] = (
                mm(self.po[f], wot[...], NN) + mm(self.pr[f], wot_other[...], NN)
            ).astype(BF16)

            @pl.when(f != me_s)
            def _():
                seq_copy(self.rs, self.rr, self.rs_send, self.rs_recv, f).start()

        def finish(self, b, back):
            rows = pl.ds(pl.multiple_of(self.r0 + b * self.pos, 8), self.pos)
            out_ref[rows, :] = middle[rows, :] + mods_t[2:3, :] * back[b].astype(F32)

        def finish_all(self):
            self.finish(me_s, self.rs)

            @pl.loop(1, depth)
            def _(d):
                b = frame_at(d)
                seq_arrival(self.rs, self.rr, self.rs_send, self.rs_recv, b).wait_recv()
                self.finish(b, self.rr)

        def drain(self):
            @pl.loop(0, depth)
            def _(f):
                tp_copy(self.xa, self.xb, self.fx_send, self.fx_recv, f).wait_send()
                tp_copy(self.pb, self.pr, self.pb_send, self.pb_recv, f).wait_send()

                @pl.when(f != me_s)
                def _():
                    seq_copy(self.nt, self.xa, self.nt_send, self.nt_recv, f).wait_send()
                    seq_copy(self.rs, self.rr, self.rs_send, self.rs_recv, f).wait_send()

    steps = [Wave(i) for i in range(len(cuts))]
    for wave in steps:
        wave.middle_out()
    loads[5].wait()
    loads[6].wait()

    before = None
    for wave in steps:
        for batch in wave.batches():
            for d in batch:
                if d:
                    wave.forward(d)
            if before is not None:
                if batch[0] == 0:
                    for copy in wot_copies:
                        copy.wait_recv()
                for d in batch:
                    before.send_back((d + 1) % depth)
            wave.project_in(batch)

        @pl.loop(0, depth)
        def _(d):
            wave.attend(d + 1)

        before = wave

    if len(steps) == 1:
        for copy in wot_copies:
            copy.wait_recv()

    @pl.loop(0, depth)
    def _(d):
        before.send_back(d + 1)

    for wave in steps:
        wave.finish_all()

    for copy in frame_copies + term_copies + part_copies + [wot_fetch] + wot_copies:
        copy.wait_send()
    for wave in steps:
        wave.drain()


def wave_scratch(depth, pos, width, heads):
    dma = pltpu.SemaphoreType.DMA
    blocks = pltpu.VMEM((depth, pos, width), BF16)
    halves = pltpu.VMEM((depth, pos, heads * HEAD_DIM), BF16)
    return [
        blocks,
        blocks,
        blocks,
        pltpu.VMEM((3, depth, heads, HEAD_DIM, 2 * pos), BF16),
        pltpu.VMEM((heads, HEAD_DIM, 2 * pos), F32),
        halves,
        halves,
        halves,
        blocks,
        blocks,
        dma((depth,)),
        dma((depth,)),
        dma((depth,)),
        dma((depth,)),
        dma((depth,)),
        dma((depth,)),
        dma((depth,)),
        dma((depth,)),
    ]


def body(
    frames,
    timestep,
    embed_weight,
    block_weight,
    spatial_table,
    temporal_table,
    spatial_qkv,
    spatial_out,
    temporal_qkv,
    temporal_out,
):
    depth = lax.axis_size("seq")
    count, _, width = frames.shape
    local = spatial_out.shape[0]
    heads = local // HEAD_DIM
    cuts = [(0, 256), (256, count - 256)] if count == 384 else [(0, count)]
    parts = min(4, lax.axis_size("clip"))
    waves = []
    for _, rows in cuts:
        waves += wave_scratch(depth, rows // depth, width, heads)
    group = 2 * depth - 1
    vmem = pl.BlockSpec(memory_space=pltpu.VMEM)
    hbm = pl.BlockSpec(memory_space=pl.ANY)
    dma = pltpu.SemaphoreType.DMA
    result = pl.pallas_call(
        functools.partial(kernel, depth, cuts),
        out_shape=jax.ShapeDtypeStruct((count, width), F32),
        in_specs=[vmem] * 3 + [hbm] * 7,
        out_specs=vmem,
        scratch_shapes=[
            pltpu.VMEM((count, width), BF16),
            pltpu.VMEM(embed_weight.shape, BF16),
            pltpu.VMEM(block_weight.shape, BF16),
            pltpu.VMEM((3, local, width), BF16),
            pltpu.VMEM((local, width), BF16),
            pltpu.VMEM((3, local, width), BF16),
            pltpu.VMEM((local, width), BF16),
            pltpu.VMEM((count, width), BF16),
            pltpu.VMEM((3, width), F32),
            pltpu.VMEM((group, 3, width), F32),
            pltpu.VMEM((3, width), F32),
            pltpu.VMEM((3, width), F32),
            pltpu.VMEM((3, heads, HEAD_DIM, 2 * count), BF16),
            pltpu.VMEM((heads, HEAD_DIM, 2 * count), F32),
            pltpu.VMEM((count, width), BF16),
            pltpu.VMEM((count, width), BF16),
            pltpu.VMEM((count, width), F32),
            pltpu.VMEM((count, width), F32),
            dma((7,)),
            dma((group,)),
            dma((group,)),
            dma((2,)),
            dma((2,)),
            dma((2,)),
            dma((2,)),
            pltpu.VMEM((heads, 2 * count, HEAD_DIM), BF16),
            pltpu.VMEM((local, width), BF16),
            dma((parts,)),
            dma((parts,)),
            pltpu.VMEM((heads, 1, 2 * count), F32),
            pltpu.VMEM((heads, 1, 2 * count), F32),
        ]
        + waves,
        compiler_params=pltpu.CompilerParams(
            collective_id=0, has_side_effects=True, vmem_limit_bytes=58 * 1024 * 1024
        ),
    )(
        time_features(timestep),
        spatial_table,
        temporal_table,
        frames.reshape(count, width),
        embed_weight,
        block_weight,
        jnp.transpose(spatial_qkv, (1, 2, 0)),
        spatial_out,
        jnp.transpose(temporal_qkv, (1, 2, 0)),
        temporal_out,
    )
    return result.reshape(frames.shape)


def solution(mesh):
    return jax.shard_map(
        body,
        mesh=mesh,
        in_specs=(
            P("tp", ("clip", "seq"), None),
            P("clip"),
            P(),
            P(("seq", "tp"), None),
            P(),
            P(),
            P(None, None, "tp"),
            P("tp", None),
            P(None, None, "tp"),
            P("tp", None),
        ),
        out_specs=P("tp", ("clip", "seq"), None),
        check_vma=False,
    )
```

```python
import functools
import math

import jax
import jax.numpy as jnp
from jax import lax
from jax.experimental import pallas as pl
from jax.experimental.pallas import tpu as pltpu
from jax.sharding import PartitionSpec as P

HEAD_DIM = 72
FREQ = 256
F32 = jnp.float32
BF16 = jnp.bfloat16
MESH = pl.DeviceIdType.MESH
NT = (((1,), (1,)), ((), ()))
TN = (((0,), (0,)), ((), ()))
NN = (((1,), (0,)), ((), ()))
WAVE_REFS = 18
FACTOR = 1.0 / math.sqrt(HEAD_DIM)
FACTOR2 = FACTOR * math.log2(math.e)


def time_features(timestep):
    half = FREQ // 2
    ladder = jnp.exp(-math.log(10000.0) * jnp.arange(half, dtype=jnp.float32) / half)
    angles = timestep.astype(jnp.float32)[:, None] * ladder[None, :]
    return jnp.concatenate([jnp.cos(angles), jnp.sin(angles)], axis=-1)


def mm(a, b, dims):
    return lax.dot_general(a, b, dims, preferred_element_type=F32)


def split_rows(row):
    wide = jnp.broadcast_to(row, (8, row.shape[1]))
    first = wide.astype(BF16).astype(F32)
    rest = wide - first
    second = rest.astype(BF16).astype(F32)
    third = rest - second
    index = lax.broadcasted_iota(jnp.int32, wide.shape, 0)
    zero = jnp.zeros_like(wide)
    return jnp.where(
        index == 0, first, jnp.where(index == 1, second, jnp.where(index == 2, third, zero))
    ).astype(BF16)


def normalise(values, scale, shift):
    width = values.shape[1]
    mean = jnp.sum(values, axis=1, keepdims=True) * (1.0 / width)
    centred = values - mean
    variance = jnp.sum(centred * centred, axis=1, keepdims=True) * (1.0 / width)
    return (centred * lax.rsqrt(variance + 1e-06) * (1.0 + scale) + shift).astype(BF16)


def kernel(
    depth,
    cuts,
    feats_ref,
    table_s,
    table_t,
    frames_hbm,
    embed_hbm,
    block_hbm,
    wqs_hbm,
    wos_hbm,
    wqt_hbm,
    wot_hbm,
    out_ref,
    frames,
    embed,
    block,
    wqs,
    wos,
    wqt,
    wot,
    theirs,
    term,
    terms,
    mods_s,
    mods_t,
    qkv,
    att,
    part_send,
    part_recv,
    own,
    middle,
    load_sem,
    term_send,
    term_recv,
    fr_send,
    fr_recv,
    part_ss,
    part_rs,
    keys,
    wot_other,
    wx_send,
    wx_recv,
    *waves,
):
    me_s = lax.axis_index("seq")
    me_t = lax.axis_index("tp")
    peer_t = 1 - me_t
    count, width = frames.shape
    heads = qkv.shape[1]
    waves = [waves[i * WAVE_REFS : (i + 1) * WAVE_REFS] for i in range(len(cuts))]

    loads = []
    for i, (src, dst) in enumerate(
        [
            (embed_hbm, embed),
            (block_hbm, block),
            (frames_hbm, frames),
            (wqs_hbm, wqs),
            (wos_hbm, wos),
            (wqt_hbm, wqt),
            (wot_hbm, wot),
        ]
    ):
        copy = pltpu.make_async_copy(src, dst, load_sem.at[i])
        copy.start()
        loads.append(copy)

    barrier = pltpu.get_barrier_semaphore()
    peers = [(ds, dt) for ds in range(depth) for dt in range(2) if ds or dt]
    for ds, dt in peers:
        pl.semaphore_signal(
            barrier,
            inc=1,
            device_id={"seq": lax.rem(me_s + ds, depth), "tp": lax.rem(me_t + dt, 2)},
            device_id_type=MESH,
        )
    parts = wx_send.shape[0]
    me_c = lax.axis_index("clip")
    piece = lax.rem(me_c, parts)
    for k in range(1, parts):
        pl.semaphore_signal(
            barrier,
            inc=1,
            device_id={"clip": me_c - piece + lax.rem(piece + k, parts)},
            device_id_type=MESH,
        )
    pl.semaphore_wait(barrier, len(peers) + parts - 1)

    frame_copies = []
    for i, (r0, n) in enumerate(cuts):
        copy = pltpu.make_async_remote_copy(
            src_ref=frames_hbm.at[pl.ds(r0, n)],
            dst_ref=theirs.at[pl.ds(r0, n)],
            send_sem=fr_send.at[i],
            recv_sem=fr_recv.at[i],
            device_id={"tp": peer_t},
            device_id_type=MESH,
        )
        copy.start()
        frame_copies.append(copy)

    loads[0].wait()
    hidden = mm(split_rows(feats_ref[...]), embed[...], NN)
    hidden = hidden[0:1] + hidden[1:2] + hidden[2:3]
    hidden = hidden / (1.0 + jnp.exp(-hidden))
    share = block.shape[0]
    start = (me_s * 2 + me_t) * share
    chosen = (
        lax.broadcasted_iota(jnp.int32, (width, share), 0)
        == lax.broadcasted_iota(jnp.int32, (width, share), 1) + start
    )
    mine = mm(split_rows(hidden), chosen.astype(F32).astype(BF16), NN).astype(BF16)
    loads[1].wait()
    spread = mm(mine, block[...], NN)
    spread = spread[0:1] + spread[1:2] + spread[2:3]
    for i in range(3):
        term[i : i + 1, :] = spread[:, i * width : (i + 1) * width]
    term_copies = []
    for i, (ds, dt) in enumerate(peers):
        copy = pltpu.make_async_remote_copy(
            src_ref=term,
            dst_ref=terms.at[i],
            send_sem=term_send.at[i],
            recv_sem=term_recv.at[i],
            device_id={"seq": lax.rem(me_s + ds, depth), "tp": lax.rem(me_t + dt, 2)},
            device_id_type=MESH,
        )
        copy.start()
        term_copies.append(copy)
    total = term[...]
    for i, copy in enumerate(term_copies):
        copy.wait_recv()
        total = total + terms[i]
    mods_s[...] = table_s[...] + total
    mods_t[...] = table_t[...] + total

    def spatial_in(tokens, r0, n, c0):
        normed = jnp.concatenate(
            [
                normalise(
                    tokens[pl.ds(r0 + k, 128), :].astype(F32), mods_s[1:2, :], mods_s[0:1, :]
                )
                for k in range(0, n, 128)
            ],
            axis=0,
        )

        @pl.loop(0, 3)
        def _(j):
            rows = mm(wqs[j], normed, NT).reshape(heads, HEAD_DIM, n)
            qkv[j, :, :, pl.ds(c0, n)] = rows.astype(BF16)

            @pl.when(j == 1)
            def _():
                for h in range(heads):
                    keys[h, pl.ds(c0, n), :] = rows[h].T.astype(BF16)

    loads[2].wait()
    loads[3].wait()
    for r0, n in cuts:
        spatial_in(frames, r0, n, r0)
    for i, (r0, n) in enumerate(cuts):
        frame_copies[i].wait_recv()
        if i == len(cuts) - 1:
            slice_rows = wot.shape[0] // parts
            wot_rows = pl.ds(pl.multiple_of(piece * slice_rows, 16), slice_rows)
            wot_fetch = pltpu.make_async_remote_copy(
                src_ref=wot_hbm.at[wot_rows],
                dst_ref=wot_other.at[wot_rows],
                send_sem=wx_send.at[0],
                recv_sem=wx_recv.at[0],
                device_id={"tp": peer_t},
                device_id_type=MESH,
            )
            wot_fetch.start()
        spatial_in(theirs, r0, n, count + r0)

    def attend(c0, n):
        @pl.loop(0, heads)
        def _(h):
            scores = mm(keys[h], qkv[0, h, :, pl.ds(c0, n)], NN)
            peak = jnp.max(scores, axis=0, keepdims=True)
            raised = jnp.exp2((scores - peak) * FACTOR2)
            norm = jnp.sum(raised, axis=0, keepdims=True)
            att[h, :, pl.ds(c0, n)] = mm(qkv[2, h], raised.astype(BF16), NN) / norm

    def project(c0, n):
        heads_out = att[:, :, pl.ds(c0, n)].reshape(heads * HEAD_DIM, n).astype(BF16)
        return mm(heads_out, wos[...], TN)

    loads[4].wait()
    part_copies = []
    for i, (r0, n) in enumerate(cuts):
        attend(count + r0, n)
        for k in range(r0, r0 + n, 128):
            part_send[pl.ds(k, 128), :] = project(count + k, 128).astype(BF16)
        copy = pltpu.make_async_remote_copy(
            src_ref=part_send.at[pl.ds(r0, n)],
            dst_ref=part_recv.at[pl.ds(r0, n)],
            send_sem=part_ss.at[i],
            recv_sem=part_rs.at[i],
            device_id={"tp": peer_t},
            device_id_type=MESH,
        )
        copy.start()
        part_copies.append(copy)
    wot_fetch.wait_recv()
    wot_copies = []
    for k in range(1, parts):
        copy = pltpu.make_async_remote_copy(
            src_ref=wot_other.at[wot_rows],
            dst_ref=wot_other.at[wot_rows],
            send_sem=wx_send.at[k],
            recv_sem=wx_recv.at[k],
            device_id={"clip": me_c - piece + lax.rem(piece + k, parts)},
            device_id_type=MESH,
        )
        copy.start()
        wot_copies.append(copy)
    for r0, n in cuts:
        attend(r0, n)
    for k in range(0, count, 128):
        own[pl.ds(k, 128), :] = project(k, 128)

    def seq_copy(src, dst, send, recv, there):
        return pltpu.make_async_remote_copy(
            src_ref=src.at[there],
            dst_ref=dst.at[me_s],
            send_sem=send.at[there],
            recv_sem=recv.at[me_s],
            device_id={"seq": there},
            device_id_type=MESH,
        )

    def seq_arrival(src, dst, send, recv, there):
        return pltpu.make_async_remote_copy(
            src_ref=src.at[there],
            dst_ref=dst.at[there],
            send_sem=send.at[there],
            recv_sem=recv.at[there],
            device_id={"seq": there},
            device_id_type=MESH,
        )

    def tp_copy(src, dst, send, recv, f):
        return pltpu.make_async_remote_copy(
            src_ref=src.at[f],
            dst_ref=dst.at[f],
            send_sem=send.at[f],
            recv_sem=recv.at[f],
            device_id={"tp": peer_t},
            device_id_type=MESH,
        )

    def frame_at(d):
        return lax.rem(me_s + d, depth)

    class Wave:
        def __init__(self, i):
            self.i = i
            self.r0, self.n = cuts[i]
            self.pos = self.n // depth
            (
                self.nt,
                self.xa,
                self.xb,
                self.qkvt,
                self.attt,
                self.pb,
                self.pr,
                self.po,
                self.rs,
                self.rr,
                self.nt_send,
                self.nt_recv,
                self.fx_send,
                self.fx_recv,
                self.pb_send,
                self.pb_recv,
                self.rs_send,
                self.rs_recv,
            ) = waves[i]

        def middle_out(self):
            part_copies[self.i].wait_recv()
            for k in range(self.r0, self.r0 + self.n, 128):
                rows = pl.ds(k, 128)
                middle[rows, :] = frames[rows, :].astype(F32) + mods_s[2:3, :] * (
                    own[rows, :] + part_recv[rows, :].astype(F32)
                )

            @pl.loop(1, depth + 1)
            def _(d):
                b = frame_at(d)
                rows = pl.ds(pl.multiple_of(self.r0 + b * self.pos, 8), self.pos)
                self.nt[b] = normalise(middle[rows, :], mods_t[1:2, :], mods_t[0:1, :])

                @pl.when(d < depth)
                def _():
                    seq_copy(self.nt, self.xa, self.nt_send, self.nt_recv, b).start()

            self.xa[me_s] = self.nt[me_s]
            tp_copy(self.xa, self.xb, self.fx_send, self.fx_recv, me_s).start()

        def forward(self, d):
            f = frame_at(d)
            seq_arrival(self.nt, self.xa, self.nt_send, self.nt_recv, f).wait_recv()
            tp_copy(self.xa, self.xb, self.fx_send, self.fx_recv, f).start()

        def batches(self):
            size = min(depth, max(1, 256 // (2 * self.pos)))
            return [range(d, min(d + size, depth)) for d in range(0, depth, size)]

        def project_in(self, batch):
            parts = []
            for d in batch:
                f = frame_at(d)
                tp_copy(self.xa, self.xb, self.fx_send, self.fx_recv, f).wait_recv()
                parts += [self.xa[f], self.xb[f]]
            if self.pos % 16:
                parts = [part.astype(F32) for part in parts]
            tokens = jnp.concatenate(parts, axis=0).astype(BF16)
            span = 2 * self.pos
            for j in range(3):
                rows = mm(wqt[j], tokens, NT).reshape(heads, HEAD_DIM, -1)
                for k, d in enumerate(batch):
                    self.qkvt[j, frame_at(d)] = rows[:, :, k * span : (k + 1) * span].astype(BF16)

        def attend(self, d):
            f = frame_at(d)
            scores = []
            for g in range(depth):
                scores.append([])
            for h in range(heads):
                query = self.qkvt[0, f, h].astype(F32)
                for g in range(depth):
                    key = self.qkvt[1, g, h].astype(F32)
                    scores[g].append(jnp.sum(query * key, axis=0, keepdims=True))
            scores = [jnp.concatenate(rows, axis=0) * FACTOR for rows in scores]
            peak = functools.reduce(jnp.maximum, scores)
            raised = [jnp.exp(s - peak) for s in scores]
            norm = functools.reduce(jnp.add, raised)
            weights = [(r / norm).astype(BF16).astype(F32) for r in raised]
            for h in range(heads):
                result = None
                for g in range(depth):
                    piece = weights[g][h : h + 1, :] * self.qkvt[2, g, h].astype(F32)
                    result = piece if result is None else result + piece
                self.attt[h] = result
            flat = self.attt[...].reshape(heads * HEAD_DIM, 2 * self.pos).T
            self.pb[f] = flat[self.pos :].astype(BF16)
            tp_copy(self.pb, self.pr, self.pb_send, self.pb_recv, f).start()
            self.po[f] = flat[: self.pos].astype(BF16)

        def send_back(self, d):
            f = frame_at(d)
            tp_copy(self.pb, self.pr, self.pb_send, self.pb_recv, f).wait_recv()
            self.rs[f] = (
                mm(self.po[f], wot[...], NN) + mm(self.pr[f], wot_other[...], NN)
            ).astype(BF16)

            @pl.when(f != me_s)
            def _():
                seq_copy(self.rs, self.rr, self.rs_send, self.rs_recv, f).start()

        def finish(self, b, back):
            rows = pl.ds(pl.multiple_of(self.r0 + b * self.pos, 8), self.pos)
            out_ref[rows, :] = middle[rows, :] + mods_t[2:3, :] * back[b].astype(F32)

        def finish_all(self):
            self.finish(me_s, self.rs)

            @pl.loop(1, depth)
            def _(d):
                b = frame_at(d)
                seq_arrival(self.rs, self.rr, self.rs_send, self.rs_recv, b).wait_recv()
                self.finish(b, self.rr)

        def drain(self):
            @pl.loop(0, depth)
            def _(f):
                tp_copy(self.xa, self.xb, self.fx_send, self.fx_recv, f).wait_send()
                tp_copy(self.pb, self.pr, self.pb_send, self.pb_recv, f).wait_send()

                @pl.when(f != me_s)
                def _():
                    seq_copy(self.nt, self.xa, self.nt_send, self.nt_recv, f).wait_send()
                    seq_copy(self.rs, self.rr, self.rs_send, self.rs_recv, f).wait_send()

    steps = [Wave(i) for i in range(len(cuts))]
    for wave in steps:
        wave.middle_out()
    loads[5].wait()
    loads[6].wait()

    before = None
    for wave in steps:
        for batch in wave.batches():
            for d in batch:
                if d:
                    wave.forward(d)
            if before is not None:
                if batch[0] == 0:
                    for copy in wot_copies:
                        copy.wait_recv()
                for d in batch:
                    before.send_back((d + 1) % depth)
            wave.project_in(batch)

        @pl.loop(0, depth)
        def _(d):
            wave.attend(d + 1)

        before = wave

    if len(steps) == 1:
        for copy in wot_copies:
            copy.wait_recv()

    @pl.loop(0, depth)
    def _(d):
        before.send_back(d + 1)

    for wave in steps:
        wave.finish_all()

    for copy in frame_copies + term_copies + part_copies + [wot_fetch] + wot_copies:
        copy.wait_send()
    for wave in steps:
        wave.drain()


def wave_scratch(depth, pos, width, heads):
    dma = pltpu.SemaphoreType.DMA
    blocks = pltpu.VMEM((depth, pos, width), BF16)
    halves = pltpu.VMEM((depth, pos, heads * HEAD_DIM), BF16)
    return [
        blocks,
        blocks,
        blocks,
        pltpu.VMEM((3, depth, heads, HEAD_DIM, 2 * pos), BF16),
        pltpu.VMEM((heads, HEAD_DIM, 2 * pos), F32),
        halves,
        halves,
        halves,
        blocks,
        blocks,
        dma((depth,)),
        dma((depth,)),
        dma((depth,)),
        dma((depth,)),
        dma((depth,)),
        dma((depth,)),
        dma((depth,)),
        dma((depth,)),
    ]


def body(
    frames,
    timestep,
    embed_weight,
    block_weight,
    spatial_table,
    temporal_table,
    spatial_qkv,
    spatial_out,
    temporal_qkv,
    temporal_out,
):
    depth = lax.axis_size("seq")
    count, _, width = frames.shape
    local = spatial_out.shape[0]
    heads = local // HEAD_DIM
    cuts = [(0, 256), (256, count - 256)] if count == 384 else [(0, count)]
    parts = min(4, lax.axis_size("clip"))
    waves = []
    for _, rows in cuts:
        waves += wave_scratch(depth, rows // depth, width, heads)
    group = 2 * depth - 1
    vmem = pl.BlockSpec(memory_space=pltpu.VMEM)
    hbm = pl.BlockSpec(memory_space=pl.ANY)
    dma = pltpu.SemaphoreType.DMA
    result = pl.pallas_call(
        functools.partial(kernel, depth, cuts),
        out_shape=jax.ShapeDtypeStruct((count, width), F32),
        in_specs=[vmem] * 3 + [hbm] * 7,
        out_specs=vmem,
        scratch_shapes=[
            pltpu.VMEM((count, width), BF16),
            pltpu.VMEM(embed_weight.shape, BF16),
            pltpu.VMEM(block_weight.shape, BF16),
            pltpu.VMEM((3, local, width), BF16),
            pltpu.VMEM((local, width), BF16),
            pltpu.VMEM((3, local, width), BF16),
            pltpu.VMEM((local, width), BF16),
            pltpu.VMEM((count, width), BF16),
            pltpu.VMEM((3, width), F32),
            pltpu.VMEM((group, 3, width), F32),
            pltpu.VMEM((3, width), F32),
            pltpu.VMEM((3, width), F32),
            pltpu.VMEM((3, heads, HEAD_DIM, 2 * count), BF16),
            pltpu.VMEM((heads, HEAD_DIM, 2 * count), F32),
            pltpu.VMEM((count, width), BF16),
            pltpu.VMEM((count, width), BF16),
            pltpu.VMEM((count, width), F32),
            pltpu.VMEM((count, width), F32),
            dma((7,)),
            dma((group,)),
            dma((group,)),
            dma((2,)),
            dma((2,)),
            dma((2,)),
            dma((2,)),
            pltpu.VMEM((heads, 2 * count, HEAD_DIM), BF16),
            pltpu.VMEM((local, width), BF16),
            dma((parts,)),
            dma((parts,)),
        ]
        + waves,
        compiler_params=pltpu.CompilerParams(
            collective_id=0, has_side_effects=True, vmem_limit_bytes=58 * 1024 * 1024
        ),
    )(
        time_features(timestep),
        spatial_table,
        temporal_table,
        frames.reshape(count, width),
        embed_weight,
        block_weight,
        jnp.transpose(spatial_qkv, (1, 2, 0)),
        spatial_out,
        jnp.transpose(temporal_qkv, (1, 2, 0)),
        temporal_out,
    )
    return result.reshape(frames.shape)


def solution(mesh):
    return jax.shard_map(
        body,
        mesh=mesh,
        in_specs=(
            P("tp", ("clip", "seq"), None),
            P("clip"),
            P(),
            P(("seq", "tp"), None),
            P(),
            P(),
            P(None, None, "tp"),
            P("tp", None),
            P(None, None, "tp"),
            P("tp", None),
        ),
        out_specs=P("tp", ("clip", "seq"), None),
        check_vma=False,
    )
```
